512 devices in a mesh: dp: 8 (over z_lo, core), axial: 64 (over x, y, z_hi).
Axes of the slice: x: 4, y: 4, z: 16 (z_hi: 4, z_lo: 4; z = z_hi * 4 + z_lo), core: 2. Of those that a mesh axis runs over, the one named last changes fastest.
Arguments:
- pair: float32 [1024, 128, 128], P(('dp', 'axial')), parts along dimension 0, may hold values from -36 to 36
- cotangent: float32 [1024, 128, 128], P(('dp', 'axial')), parts along dimension 0, may hold values from -16 to 16
- norm_gain: float32 [2, 128], replicated, may hold values from 0.5 to 1.5
- norm_shift: float32 [2, 128], replicated, may hold values from -3 to 3
- weight_in: float32 [2, 128, 512], replicated, may hold values from -0.5 to 0.5
- weight_bias: float32 [2, 128, 4], replicated, may hold values from -0.5 to 0.5
- gate_shift: float32 [2, 128], replicated, may hold values from -4 to 4
- weight_out: float32 [2, 128, 128], replicated, may hold values from -0.5 to 0.5
Outputs:
- final: float32 [1024, 128, 128], P(('dp', 'axial')), parts along dimension 0
- grad_pair: float32 [1024, 128, 128], P(('dp', 'axial')), parts along dimension 0
- grad_in: float32 [16, 128, 512], P('dp'), parts along dimension 0
- grad_bias: float32 [16, 128, 4], P('dp'), parts along dimension 0
- grad_out: float32 [16, 128, 128], P('dp'), parts along dimension 0
The draws below stay inside these ranges and needn't reach their ends.
There are 8 independent parts, one for each index of `dp`. The reference program is written for one: setup_inputs(seed, part) draws one part's arguments, and reference() takes and returns one part's arrays. A program takes and returns all parts, laid end to end along the dimension named above; an argument that names none is the same for every part. Nothing has to cross between parts.
All inputs are finite; a program needn't handle non-finite values.
Results may differ from the reference program's by a relative error of at most 0.00014.
Values sent between devices are 32-bit elements; how exact they have to be, the bound alone decides.
No kernel may reach another device: no remote copies, remote signals or barrier semaphores. Data moves between devices by JAX's collectives and lax.ppermute only.
A program may use at most 64 MiB of HBM per device.

```python
import math
import jax
import jax.numpy as jnp
from jax import lax

C = 128
HEADS = 4
N = 128


def draw_pair(key, part):
    key = jax.random.fold_in(key, 11)
    keys_list = jax.random.split(key, 3)
    entry_scale = jnp.exp(jax.random.uniform(keys_list[0], (N, N, 1), jnp.float32, math.log(0.3), math.log(3.0)))
    channel_scale = jnp.exp(jax.random.uniform(keys_list[1], (1, 1, C), jnp.float32, math.log(0.3), math.log(3.0)))
    base = jnp.clip(jax.random.normal(keys_list[2], (N, N, C), jnp.float32), -4.0, 4.0)
    return base * entry_scale * channel_scale


def with_spikes(values, stream_key, source, target, parts, factor):
    owner, partner = [(jnp.arange(values.shape[dim]) // (values.shape[dim] // parts)).reshape([-1 if axis == dim else 1 for axis in range(values.ndim)]) for dim in (source, target)]
    chosen = jax.random.permutation(stream_key, parts)[partner]
    strong = (owner == chosen) | (owner == (partner + parts // 2) % parts)
    return jnp.where(strong, factor * values, values)


def block_levels(own_key, dims, cuts, low, high):
    factor_of = 1.0
    for position, blocks in cuts:
        heights = jax.random.uniform(jax.random.fold_in(jax.random.fold_in(own_key, 6), position), (blocks,), jnp.float32, low / len(cuts), high / len(cuts))
        factor_of = factor_of * jnp.repeat(jnp.exp(heights), dims[position] // blocks).reshape((-1,) + (1,) * (len(dims) - 1 - position))
    return factor_of


def scatter_about(rng, extent, scale, most, cuts=(), dtype=jnp.bfloat16):
    loudness = block_levels(rng, extent, cuts, -0.22, 0.18) if cuts else 1.0
    result = jax.random.normal(rng, extent, jnp.float32) * scale * loudness
    return jnp.minimum(jnp.maximum(result, -most), most).astype(dtype)


def noise_with(stream_key, shape, scale, reach, pieces, heavy, held_as=jnp.bfloat16):
    result = scale * jax.random.normal(stream_key, shape, jnp.float32)
    if pieces:
        result = result * block_levels(stream_key, shape, pieces, -0.22, 0.18)
    return jnp.clip(with_spikes(result, jax.random.fold_in(stream_key, 3), *heavy), -reach, reach).astype(held_as)


def setup_inputs(seed: int = 0, part: int = 0) -> dict:
    arg_keys = jax.random.split(jax.random.key(seed), 9)
    part_keys = jax.random.split(jax.random.fold_in(arg_keys[8], part), 9)
    return {
        "pair": draw_pair(jax.random.fold_in(jax.random.fold_in(arg_keys[8], part), 71), part),
        "cotangent": noise_with(part_keys[1], (N, N, C), 1.0, 16.0, ((0, 64),), (0, 1, 64, 4.0), jnp.float32),
        "norm_gain": jnp.clip(jax.random.uniform(arg_keys[2], (2, C), jnp.float32, 0.5, 1.5), 0.5, 1.5),
        "norm_shift": scatter_about(arg_keys[3], (2, C), 0.5, 3.0, (), jnp.float32),
        "weight_in": scatter_about(arg_keys[4], (2, C, 4 * C), C ** -0.5, 0.5, (), jnp.float32),
        "weight_bias": scatter_about(arg_keys[5], (2, C, HEADS), C ** -0.5, 0.5, (), jnp.float32),
        "gate_shift": scatter_about(arg_keys[6], (2, C), 1.0, 4.0, (), jnp.float32),
        "weight_out": scatter_about(arg_keys[7], (2, C, C), C ** -0.5, 0.5, (), jnp.float32),
    }


highest = lax.Precision.HIGHEST

def normed(pair_in, norm_gain, norm_shift):
    centre = pair_in - lax.optimization_barrier(jnp.mean(pair_in, axis=-1, keepdims=True))
    spread = lax.optimization_barrier(jnp.mean(centre * centre, axis=-1, keepdims=True))
    return centre * lax.rsqrt(spread + 1e-05) * norm_gain + norm_shift

def pair_bias(pair_in, norm_gain, norm_shift, weight_bias):
    return jnp.einsum('rjc,ch->rjh', normed(pair_in, norm_gain, norm_shift), weight_bias, precision=highest)

def attend(pair_in, norm_gain, norm_shift, weight_in, gate_shift, weight_out, bias_full):
    row_count, col_count, channels = pair_in.shape
    head_count = bias_full.shape[-1]
    head_size = channels // head_count
    normal_in = normed(pair_in, norm_gain, norm_shift)
    projected = jnp.einsum('rjc,ce->rje', normal_in, weight_in, precision=highest)
    queries, keys_all, values_all, gate_raw = jnp.split(projected, 4, axis=-1)
    split_shape = (row_count, col_count, head_count, head_size)
    queries = queries.reshape(split_shape)
    keys_all = keys_all.reshape(split_shape)
    values_all = values_all.reshape(split_shape)
    logits = jnp.einsum('rjhd,rkhd->rhjk', queries, keys_all, precision=highest) * head_size ** (-0.5)
    logits = logits + jnp.transpose(bias_full, (2, 0, 1))[None]
    exponent = jnp.exp(logits)
    attention = exponent / lax.optimization_barrier(jnp.sum(exponent, axis=-1, keepdims=True))
    mixture = jnp.einsum('rhjk,rkhd->rjhd', attention, values_all, precision=highest).reshape(row_count, col_count, channels)
    gated_out = jax.nn.sigmoid(gate_raw + gate_shift) * mixture
    return pair_in + jnp.einsum('rjc,cd->rjd', gated_out, weight_out, precision=highest)

def module_apply(pair_in, norm_gain, norm_shift, weight_in, weight_bias, gate_shift, weight_out):
    bias_full = pair_bias(pair_in, norm_gain, norm_shift, weight_bias)

    def one_row(row_in):
        return attend(row_in[None], norm_gain, norm_shift, weight_in, gate_shift, weight_out, bias_full)[0]
    return lax.map(jax.checkpoint(one_row), pair_in)

def reference(pair, cotangent, norm_gain, norm_shift, weight_in, weight_bias, gate_shift, weight_out):

    def forward(pair_in, w_inner, w_biases, w_outer):
        first = module_apply(pair_in, norm_gain[0], norm_shift[0], w_inner[0], w_biases[0], gate_shift[0], w_outer[0])
        flipped = jnp.transpose(first, (1, 0, 2))
        second = module_apply(flipped, norm_gain[1], norm_shift[1], w_inner[1], w_biases[1], gate_shift[1], w_outer[1])
        return jnp.transpose(second, (1, 0, 2))
    final, backward = jax.vjp(forward, pair, weight_in, weight_bias, weight_out)
    grad_pair, grad_in, grad_bias, grad_out = backward(cotangent)
    factor = 1.0 / pair.shape[0]
    return (final, grad_pair, grad_in * factor, grad_bias * factor, grad_out * factor)
```

```python
import jax
import jax.numpy as jnp
from jax import lax
from jax.experimental import pallas as pl
from jax.experimental.pallas import tpu as pltpu
from jax.sharding import PartitionSpec as P

f32 = jnp.float32
both = ("dp", "axial")
homes = (
    (5, (2, 0, 1, 3)),
    (7, (2, 3, 0, 1)),
    (1, (0, 2, 3, 1)),
    (3, (0, 1, 2, 3)),
    (6, (2, 0, 1, 3)),
    (0, (2, 3, 0, 1)),
    (4, (0, 1, 2, 3)),
    (2, (0, 2, 3, 1)),
)


def compact_id(part, rank):
    block, places = homes[part]
    place = places[rank % 4]
    z = 2 * block + place // 2
    return ((z % 4) * 2 + place % 2) * 64 + (rank // 4) * 4 + z // 4


def plans(mesh):
    parts, size = mesh.shape["dp"], mesh.shape["axial"]
    if (parts, size) == (8, 64):
        placed = [[compact_id(c, r) for r in range(64)] for c in range(8)]
    else:
        placed = [[c * size + r for r in range(size)] for c in range(parts)]
    there = [(c * size + r, placed[c][r]) for c in range(parts) for r in range(size)]
    back = [(b, a) for a, b in there]
    fours = [ids[4 * b : 4 * b + 4] for ids in placed for b in range(16)]
    planes = [[c * size + 4 * b + k for b in range(16)] for c in range(parts) for k in range(4)]
    return placed, there, back, fours, planes


def dot(a, b, ca, cb):
    return lax.dot_general(
        a, b, (((ca,), (cb,)), ((), ())), precision=lax.Precision.HIGH, preferred_element_type=f32
    )


def norm_parts(x):
    centre = x - jnp.mean(x, axis=-1, keepdims=True)
    root = lax.rsqrt(jnp.mean(centre * centre, axis=-1, keepdims=True) + 1e-05)
    return centre * root, root


def norm_back(dy, gain, unit, root):
    du = dy * gain
    return root * (
        du
        - jnp.mean(du, axis=-1, keepdims=True)
        - unit * jnp.mean(du * unit, axis=-1, keepdims=True)
    )


def by_head(a):
    lane = lax.broadcasted_iota(jnp.int32, a.shape, 1) // 32
    return jnp.concatenate([jnp.where(lane == h, a, 0.0) for h in range(4)], axis=0)


def side_by_side(a):
    return jnp.concatenate([a[128 * h : 128 * h + 128] for h in range(4)], axis=1)


SCALE = 32**-0.5


def probabilities(q, k, bias, keys_down):
    if keys_down:
        e = jnp.exp(dot(by_head(k), q, 1, 1) * SCALE + bias)
        total = jnp.sum(e.reshape(4, 128, 128), axis=1, keepdims=True)
        return (e.reshape(4, 128, 128) * (1.0 / total)).reshape(512, 128)
    e = jnp.exp(dot(by_head(q), k, 1, 1) * SCALE + bias)
    return e * (1.0 / jnp.sum(e, axis=1, keepdims=True))


def mix(probs, v, keys_down):
    if keys_down:
        return dot(probs, by_head(v), 0, 0)
    return dot(side_by_side(probs), by_head(v), 1, 0)


def attention_back(do, q, k, v, probs, keys_down):
    if keys_down:
        dp = dot(by_head(v), do, 1, 1)
        both_p = (probs * dp).reshape(4, 128, 128)
        ds = (both_p - probs.reshape(4, 128, 128) * jnp.sum(both_p, axis=1, keepdims=True)).reshape(
            512, 128
        )
        dv = dot(side_by_side(probs), by_head(do), 1, 0)
        dk = dot(side_by_side(ds), by_head(q), 1, 0) * SCALE
        dq = dot(ds, by_head(k), 0, 0) * SCALE
    else:
        dp = dot(by_head(do), v, 1, 1)
        both_p = probs * dp
        ds = both_p - probs * jnp.sum(both_p, axis=1, keepdims=True)
        dv = dot(probs, by_head(do), 0, 0)
        dk = dot(ds, by_head(q), 0, 0) * SCALE
        dq = dot(side_by_side(ds), by_head(k), 1, 0) * SCALE
    return ds, dq, dk, dv


def gather_rows(ref, first, stride):
    a, b = first
    return jnp.concatenate([ref[pl.ds(a, 64, stride=stride), :], ref[pl.ds(b, 64, stride=stride), :]])


def scatter_rows(ref, first, stride, value):
    a, b = first
    ref[pl.ds(a, 64, stride=stride), :] = value[:64]
    ref[pl.ds(b, 64, stride=stride), :] = value[64:]


def start_kernel(xin, gain, shift, wbias, out):
    rows = []
    for r in range(2):
        x = gather_rows(xin, (r * 128, r * 128 + 1), 2)
        unit, root = norm_parts(x)
        rows.append(dot(wbias[0], unit * gain[0:1, :] + shift[0:1, :], 1, 1))
    block = jnp.concatenate(rows, axis=0)
    for q in range(64):
        out[q * 8 : q * 8 + 8, :] = block


def first_kernel(
    xin, brecv, gain, shift, win, wbias, gate, wout, send, proj_o, probs_o, mixed_o, first_o
):
    bias = jnp.concatenate([gather_rows(brecv, (h, 4 + h), 8) for h in range(4)])
    x = jnp.concatenate([gather_rows(xin, (r * 128, r * 128 + 1), 2) for r in range(2)])
    unit, root = norm_parts(x)
    proj = dot(unit * gain[0:1, :] + shift[0:1, :], win[0], 1, 0)
    proj_o[...] = proj
    mixed = []
    for r in range(2):
        part = proj[r * 128 : r * 128 + 128]
        probs = probabilities(part[:, 0:128], part[:, 128:256], bias, False)
        probs_o[r * 512 : r * 512 + 512, :] = probs
        mixed.append(mix(probs, part[:, 256:384], False))
    mixed = jnp.concatenate(mixed)
    mixed_o[...] = mixed
    gated = jax.nn.sigmoid(proj[:, 384:512] + gate[0:1, :]) * mixed
    first = x + dot(gated, wout[0], 1, 0)
    first_o[...] = first
    unit1, root1 = norm_parts(first)
    y1 = unit1 * gain[1:2, :] + shift[1:2, :]
    bias_rows = jnp.concatenate(
        [dot(wbias[1], y1[r * 128 : r * 128 + 128], 1, 1) for r in range(2)], axis=0
    )
    for q in range(64):
        send[q * 16 + 4 : q * 16 + 12, :] = bias_rows
    for r in range(2):
        scatter_rows(send, (r * 2, r * 2 + 1), 16, first[r * 128 : r * 128 + 128])
        cot = gather_rows(xin, (256 + r * 128, 256 + r * 128 + 1), 2)
        scatter_rows(send, (12 + r * 2, 12 + r * 2 + 1), 16, cot)


def second_kernel(recv, gain, shift, win, gate, wout, send, wgrad):
    bias = jnp.concatenate([gather_rows(recv, (4 + h, 8 + h), 16) for h in range(4)])
    x = jnp.concatenate([gather_rows(recv, (c, 2 + c), 16) for c in range(2)])
    up = jnp.concatenate([gather_rows(recv, (12 + c, 14 + c), 16) for c in range(2)])
    unit, root = norm_parts(x)
    y = unit * gain[1:2, :] + shift[1:2, :]
    proj = dot(y, win[1], 1, 0)
    probs, mixed = [], []
    for c in range(2):
        part = proj[c * 128 : c * 128 + 128]
        probs.append(probabilities(part[:, 0:128], part[:, 128:256], bias, True))
        mixed.append(mix(probs[c], part[:, 256:384], True))
    mixed = jnp.concatenate(mixed)
    sig = jax.nn.sigmoid(proj[:, 384:512] + gate[1:2, :])
    gated = sig * mixed
    final = x + dot(gated, wout[1], 1, 0)
    dgated = dot(up, wout[1], 1, 1)
    dout = dot(gated, up, 0, 0)
    dmixed = dgated * sig
    dgate = dgated * mixed * sig * (1.0 - sig)
    dproj, dbias = [], 0.0
    for c in range(2):
        part = proj[c * 128 : c * 128 + 128]
        ds, dq, dk, dv = attention_back(
            dmixed[c * 128 : c * 128 + 128],
            part[:, 0:128],
            part[:, 128:256],
            part[:, 256:384],
            probs[c],
            True,
        )
        dbias = dbias + ds
        dproj.append(jnp.concatenate([dq, dk, dv, dgate[c * 128 : c * 128 + 128]], axis=1))
    dproj = jnp.concatenate(dproj)
    din = dot(y, dproj, 0, 0)
    dx = up + norm_back(dot(dproj, win[1], 1, 1), gain[1:2, :], unit, root)
    for c in range(2):
        scatter_rows(send, (c, 2 + c), 16, dx[c * 128 : c * 128 + 128])
        scatter_rows(send, (12 + c, 14 + c), 16, final[c * 128 : c * 128 + 128])
    for h in range(4):
        scatter_rows(send, (4 + h, 8 + h), 16, dbias[h * 128 : h * 128 + 128])
    for e in range(4):
        wgrad[e * 128 : e * 128 + 128, :] = din[:, e * 128 : e * 128 + 128]
    wgrad[512:640, :] = dout


def third_kernel(
    recv, xin, first, proj_s, probs_s, mixed_s, wgrad, gain, shift, win, wbias, gate, wout, send, dx_o, final_o
):
    for r in range(2):
        for c in range(2):
            final_o[pl.ds(r * 128 + c, 64, stride=2), :] = recv[pl.ds(12 + 2 * r + c, 64, stride=16), :]
    summed = jnp.sum(recv[...].reshape(64, 16, 128)[:, 4:12, :], axis=0)
    unit1, root1 = norm_parts(first[...])
    y1 = unit1 * gain[1:2, :] + shift[1:2, :]
    dy1 = jnp.concatenate([dot(summed[4 * r : 4 * r + 4], wbias[1], 0, 0) for r in range(2)])
    gb1 = dot(summed[0:4], y1[:128], 1, 0) + dot(summed[4:8], y1[128:], 1, 0)
    up = jnp.concatenate([gather_rows(recv, (2 * r, 2 * r + 1), 16) for r in range(2)])
    up = up + norm_back(dy1, gain[1:2, :], unit1, root1)
    x = jnp.concatenate([gather_rows(xin, (r * 128, r * 128 + 1), 2) for r in range(2)])
    unit, root = norm_parts(x)
    y = unit * gain[0:1, :] + shift[0:1, :]
    proj = proj_s[...]
    mixed = mixed_s[...]
    sig = jax.nn.sigmoid(proj[:, 384:512] + gate[0:1, :])
    dgated = dot(up, wout[0], 1, 1)
    dout = dot(sig * mixed, up, 0, 0)
    dmixed = dgated * sig
    dgate = dgated * mixed * sig * (1.0 - sig)
    dproj, dbias = [], 0.0
    for r in range(2):
        part = proj[r * 128 : r * 128 + 128]
        ds, dq, dk, dv = attention_back(
            dmixed[r * 128 : r * 128 + 128],
            part[:, 0:128],
            part[:, 128:256],
            part[:, 256:384],
            probs_s[r * 512 : r * 512 + 512, :],
            False,
        )
        dbias = dbias + ds
        dproj.append(jnp.concatenate([dq, dk, dv, dgate[r * 128 : r * 128 + 128]], axis=1))
    dproj = jnp.concatenate(dproj)
    din = dot(y, dproj, 0, 0)
    dx_o[...] = up + norm_back(dot(dproj, win[0], 1, 1), gain[0:1, :], unit, root)
    for h in range(4):
        scatter_rows(send, (h, 4 + h), 32, dbias[h * 128 : h * 128 + 128])
    for i in range(10):
        source = din[64 * (i % 2) : 64 * (i % 2) + 64, 128 * (i // 2) : 128 * (i // 2) + 128] if i < 8 else dout[64 * (i - 8) : 64 * (i - 8) + 64]
        send[pl.ds(8 + i, 64, stride=32), :] = source
        send[pl.ds(18 + i, 64, stride=32), :] = wgrad[64 * i : 64 * i + 64, :]
    for q in range(64):
        send[q * 32 + 28 : q * 32 + 32, :] = gb1


def fourth_kernel(recv, xin, dx_s, final_s, gain, shift, wbias, shares, tail):
    total = jnp.sum(recv[...].reshape(64, 32, 128), axis=0)
    x = jnp.concatenate([gather_rows(xin, (r * 128, r * 128 + 1), 2) for r in range(2)])
    unit, root = norm_parts(x)
    y = unit * gain[0:1, :] + shift[0:1, :]
    dy = jnp.concatenate([dot(total[4 * r : 4 * r + 4], wbias[0], 0, 0) for r in range(2)])
    gb0 = dot(total[0:4], y[:128], 1, 0) + dot(total[4:8], y[128:], 1, 0)
    dx = dx_s[...] + norm_back(dy, gain[0:1, :], unit, root)
    for r in range(2):
        scatter_rows(tail, (r * 128, r * 128 + 1), 2, dx[r * 128 : r * 128 + 128])
    tail[256:512, :] = final_s[...]
    tail[512:520, :] = jnp.concatenate([total[28:32], total[28:32]], axis=0) * (1.0 / 128)
    share = jnp.concatenate([total[8:28], gb0], axis=0) * (1.0 / 128)
    for k in range(4):
        shares[24 * k : 24 * k + 24, :] = share


def last_kernel(recv, gb1, gin, gbias, gout):
    for m in range(2):
        for i in range(10):
            piece = recv[pl.ds(10 * m + i, 64, stride=24), :]
            if i < 8:
                gin[m, 64 * (i % 2) : 64 * (i % 2) + 64, 128 * (i // 2) : 128 * (i // 2) + 128] = piece
            else:
                gout[m, 64 * (i - 8) : 64 * (i - 8) + 64, :] = piece
    gbias[0] = jnp.sum(recv[...].reshape(64, 24, 128), axis=0)[20:24]
    gbias[1] = gb1[0:4]


def call(kernel, outs, *args):
    return pl.pallas_call(
        kernel,
        out_shape=tuple(jax.ShapeDtypeStruct(s, f32) for s in outs),
        in_specs=[pl.BlockSpec(memory_space=pltpu.VMEM)] * len(args),
        out_specs=tuple(pl.BlockSpec(memory_space=pltpu.VMEM) for _ in outs),
        compiler_params=pltpu.CompilerParams(vmem_limit_bytes=48 * 1024 * 1024),
    )(*args)


def solution(mesh):
    placed, there, back, fours, planes = plans(mesh)

    def swap(a, groups):
        count = len(groups[0])
        cut = a.reshape(count, a.shape[0] // count, 128)
        got = lax.all_to_all(cut, both, 0, 0, axis_index_groups=groups, tiled=True)
        return got.reshape(a.shape)

    def body(pair, cotangent, gain, shift, win, wb, gate, wout):
        wbias = jnp.transpose(wb, (0, 2, 1))
        flat = jnp.concatenate([pair.reshape(256, 128), cotangent.reshape(256, 128)])
        xin = lax.ppermute(flat, both, there)
        (bsend,) = call(start_kernel, [(512, 128)], xin, gain, shift, wbias)
        brecv = swap(bsend, placed)
        send1, proj, probs, mixed, first = call(
            first_kernel,
            [(1024, 128), (256, 512), (1024, 128), (256, 128), (256, 128)],
            *(xin, brecv, gain, shift, win, wbias, gate, wout),
        )
        recv1 = swap(send1, placed)
        send2, wgrad = call(
            second_kernel, [(1024, 128), (640, 128)], recv1, gain, shift, win, gate, wout
        )
        recv2 = swap(send2, placed)
        send3, dx, final = call(
            third_kernel,
            [(2048, 128), (256, 128), (256, 128)],
            *(recv2, xin, first, proj, probs, mixed, wgrad, gain, shift, win, wbias, gate, wout),
        )
        recv3 = swap(send3, placed)
        shares, tail = call(
            fourth_kernel,
            [(96, 128), (520, 128)],
            *(recv3, xin, dx, final, gain, shift, wbias),
        )
        tail = lax.ppermute(tail, both, back)
        shares = lax.ppermute(swap(shares, fours), both, back)
        recv4 = swap(jnp.broadcast_to(shares[None], (16, 96, 128)).reshape(1536, 128), planes)
        gin, gbias, gout = call(
            last_kernel, [(2, 128, 512), (2, 4, 128), (2, 128, 128)], recv4, tail[512:520]
        )
        return (
            tail[256:512].reshape(2, 128, 128),
            tail[0:256].reshape(2, 128, 128),
            gin,
            jnp.transpose(gbias, (0, 2, 1)),
            gout,
        )

    rows = P(("dp", "axial"), None, None)
    part = P("dp", None, None)
    return jax.shard_map(
        body,
        mesh=mesh,
        in_specs=(rows, rows, P(), P(), P(), P(), P(), P()),
        out_specs=(rows, rows, part, part, part),
        check_vma=False,
    )
```

```python
import jax
import jax.numpy as jnp
from jax import lax
from jax.experimental import pallas as pl
from jax.experimental.pallas import tpu as pltpu
from jax.sharding import PartitionSpec as P

f32 = jnp.float32
both = ("dp", "axial")
homes = (
    (5, (2, 0, 1, 3)),
    (7, (2, 3, 0, 1)),
    (1, (0, 2, 3, 1)),
    (3, (0, 1, 2, 3)),
    (6, (2, 0, 1, 3)),
    (0, (2, 3, 0, 1)),
    (4, (0, 1, 2, 3)),
    (2, (0, 2, 3, 1)),
)


def compact_id(part, rank):
    block, places = homes[part]
    place = places[rank % 4]
    z = 2 * block + place // 2
    return ((z % 4) * 2 + place % 2) * 64 + (rank // 4) * 4 + z // 4


def plans(mesh):
    parts, size = mesh.shape["dp"], mesh.shape["axial"]
    if (parts, size) == (8, 64):
        placed = [[compact_id(c, r) for r in range(64)] for c in range(8)]
    else:
        placed = [[c * size + r for r in range(size)] for c in range(parts)]
    there = [(c * size + r, placed[c][r]) for c in range(parts) for r in range(size)]
    back = [(b, a) for a, b in there]
    fours = [ids[4 * b : 4 * b + 4] for ids in placed for b in range(16)]
    planes = [[c * size + 4 * b + k for b in range(16)] for c in range(parts) for k in range(4)]
    return placed, there, back, fours, planes


def dot(a, b, ca, cb):
    return lax.dot_general(
        a, b, (((ca,), (cb,)), ((), ())), precision=lax.Precision.HIGH, preferred_element_type=f32
    )


def norm_parts(x):
    centre = x - jnp.mean(x, axis=-1, keepdims=True)
    root = lax.rsqrt(jnp.mean(centre * centre, axis=-1, keepdims=True) + 1e-05)
    return centre * root, root


def norm_back(dy, gain, unit, root):
    du = dy * gain
    return root * (
        du
        - jnp.mean(du, axis=-1, keepdims=True)
        - unit * jnp.mean(du * unit, axis=-1, keepdims=True)
    )


def by_head(a):
    lane = lax.broadcasted_iota(jnp.int32, a.shape, 1) // 32
    return jnp.concatenate([jnp.where(lane == h, a, 0.0) for h in range(4)], axis=0)


def side_by_side(a):
    return jnp.concatenate([a[128 * h : 128 * h + 128] for h in range(4)], axis=1)


SCALE = 32**-0.5


def probabilities(q, k, bias, keys_down):
    if keys_down:
        e = jnp.exp(dot(by_head(k), q, 1, 1) * SCALE + bias)
        total = jnp.sum(e.reshape(4, 128, 128), axis=1, keepdims=True)
        return (e.reshape(4, 128, 128) * (1.0 / total)).reshape(512, 128)
    e = jnp.exp(dot(by_head(q), k, 1, 1) * SCALE + bias)
    return e * (1.0 / jnp.sum(e, axis=1, keepdims=True))


def mix(probs, v, keys_down):
    if keys_down:
        return dot(probs, by_head(v), 0, 0)
    return dot(side_by_side(probs), by_head(v), 1, 0)


def attention_back(do, q, k, v, probs, keys_down):
    if keys_down:
        dp = dot(by_head(v), do, 1, 1)
        both_p = (probs * dp).reshape(4, 128, 128)
        ds = (both_p - probs.reshape(4, 128, 128) * jnp.sum(both_p, axis=1, keepdims=True)).reshape(
            512, 128
        )
        dv = dot(side_by_side(probs), by_head(do), 1, 0)
        dk = dot(side_by_side(ds), by_head(q), 1, 0) * SCALE
        dq = dot(ds, by_head(k), 0, 0) * SCALE
    else:
        dp = dot(by_head(do), v, 1, 1)
        both_p = probs * dp
        ds = both_p - probs * jnp.sum(both_p, axis=1, keepdims=True)
        dv = dot(probs, by_head(do), 0, 0)
        dk = dot(ds, by_head(q), 0, 0) * SCALE
        dq = dot(side_by_side(ds), by_head(k), 1, 0) * SCALE
    return ds, dq, dk, dv


def gather_rows(ref, first, stride):
    a, b = first
    return jnp.concatenate([ref[pl.ds(a, 64, stride=stride), :], ref[pl.ds(b, 64, stride=stride), :]])


def scatter_rows(ref, first, stride, value):
    a, b = first
    ref[pl.ds(a, 64, stride=stride), :] = value[:64]
    ref[pl.ds(b, 64, stride=stride), :] = value[64:]


def vectors(small):
    return small[0:2, :], small[2:4, :], small[4:6, :], (small[8:12, :], small[12:16, :])


def start_kernel(xin, small, out):
    gain, shift, _, wbias = vectors(small)
    rows = []
    for r in range(2):
        x = gather_rows(xin, (r * 128, r * 128 + 1), 2)
        unit, root = norm_parts(x)
        rows.append(dot(wbias[0], unit * gain[0:1, :] + shift[0:1, :], 1, 1))
    block = jnp.concatenate(rows, axis=0)
    for q in range(64):
        out[q * 8 : q * 8 + 8, :] = block


def project_kernel(xin, cot, small, win, x_o, proj_o, logits_o):
    gain, shift, _, _ = vectors(small)
    x = jnp.concatenate([gather_rows(xin, (r * 128, r * 128 + 1), 2) for r in range(2)])
    x_o[...] = x
    unit, root = norm_parts(x)
    proj = dot(unit * gain[0:1, :] + shift[0:1, :], win[0], 1, 0)
    proj_o[...] = proj
    for r in range(2):
        part = proj[r * 128 : r * 128 + 128]
        logits_o[r * 512 : r * 512 + 512, :] = (
            dot(by_head(part[:, 0:128]), part[:, 128:256], 1, 1) * SCALE
        )


def first_kernel(x, cot, brecv, proj, logits, small, wout, send, probs_o, mixed_o, first_o):
    gain, shift, gate, wbias = vectors(small)
    bias = jnp.concatenate([gather_rows(brecv, (h, 4 + h), 8) for h in range(4)])
    mixed = []
    for r in range(2):
        e = jnp.exp(logits[r * 512 : r * 512 + 512, :] + bias)
        probs = e * (1.0 / jnp.sum(e, axis=1, keepdims=True))
        probs_o[r * 512 : r * 512 + 512, :] = probs
        mixed.append(mix(probs, proj[r * 128 : r * 128 + 128, 256:384], False))
    mixed = jnp.concatenate(mixed)
    mixed_o[...] = mixed
    gated = jax.nn.sigmoid(proj[:, 384:512] + gate[0:1, :]) * mixed
    first = x[...] + dot(gated, wout[0], 1, 0)
    first_o[...] = first
    unit1, root1 = norm_parts(first)
    y1 = unit1 * gain[1:2, :] + shift[1:2, :]
    bias_rows = jnp.concatenate(
        [dot(wbias[1], y1[r * 128 : r * 128 + 128], 1, 1) for r in range(2)], axis=0
    )
    for q in range(64):
        send[q * 16 + 4 : q * 16 + 12, :] = bias_rows
    for r in range(2):
        scatter_rows(send, (r * 2, r * 2 + 1), 16, first[r * 128 : r * 128 + 128])
        rows = gather_rows(cot, (r * 128, r * 128 + 1), 2)
        scatter_rows(send, (12 + r * 2, 12 + r * 2 + 1), 16, rows)


def second_kernel(recv, small, win, wout, send, wgrad):
    gain, shift, gate, _ = vectors(small)
    bias = jnp.concatenate([gather_rows(recv, (4 + h, 8 + h), 16) for h in range(4)])
    x = jnp.concatenate([gather_rows(recv, (c, 2 + c), 16) for c in range(2)])
    up = jnp.concatenate([gather_rows(recv, (12 + c, 14 + c), 16) for c in range(2)])
    unit, root = norm_parts(x)
    y = unit * gain[1:2, :] + shift[1:2, :]
    proj = dot(y, win[1], 1, 0)
    probs, mixed = [], []
    for c in range(2):
        part = proj[c * 128 : c * 128 + 128]
        probs.append(probabilities(part[:, 0:128], part[:, 128:256], bias, True))
        mixed.append(mix(probs[c], part[:, 256:384], True))
    mixed = jnp.concatenate(mixed)
    sig = jax.nn.sigmoid(proj[:, 384:512] + gate[1:2, :])
    gated = sig * mixed
    final = x + dot(gated, wout[1], 1, 0)
    dgated = dot(up, wout[1], 1, 1)
    dout = dot(gated, up, 0, 0)
    dmixed = dgated * sig
    dgate = dgated * mixed * sig * (1.0 - sig)
    dproj, dbias = [], 0.0
    for c in range(2):
        part = proj[c * 128 : c * 128 + 128]
        ds, dq, dk, dv = attention_back(
            dmixed[c * 128 : c * 128 + 128],
            part[:, 0:128],
            part[:, 128:256],
            part[:, 256:384],
            probs[c],
            True,
        )
        dbias = dbias + ds
        dproj.append(jnp.concatenate([dq, dk, dv, dgate[c * 128 : c * 128 + 128]], axis=1))
    dproj = jnp.concatenate(dproj)
    din = dot(y, dproj, 0, 0)
    dx = up + norm_back(dot(dproj, win[1], 1, 1), gain[1:2, :], unit, root)
    for c in range(2):
        scatter_rows(send, (c, 2 + c), 16, dx[c * 128 : c * 128 + 128])
        scatter_rows(send, (12 + c, 14 + c), 16, final[c * 128 : c * 128 + 128])
    for h in range(4):
        scatter_rows(send, (4 + h, 8 + h), 16, dbias[h * 128 : h * 128 + 128])
    for e in range(4):
        wgrad[e * 128 : e * 128 + 128, :] = din[:, e * 128 : e * 128 + 128]
    wgrad[512:640, :] = dout


def third_kernel(
    recv, xin, first, proj_s, probs_s, mixed_s, wgrad, small, win, wout, send, dx_o, final_o
):
    gain, shift, gate, wbias = vectors(small)
    for r in range(2):
        for c in range(2):
            final_o[pl.ds(r * 128 + c, 64, stride=2), :] = recv[pl.ds(12 + 2 * r + c, 64, stride=16), :]
    summed = jnp.sum(recv[...].reshape(64, 16, 128)[:, 4:12, :], axis=0)
    unit1, root1 = norm_parts(first[...])
    y1 = unit1 * gain[1:2, :] + shift[1:2, :]
    dy1 = jnp.concatenate([dot(summed[4 * r : 4 * r + 4], wbias[1], 0, 0) for r in range(2)])
    gb1 = dot(summed[0:4], y1[:128], 1, 0) + dot(summed[4:8], y1[128:], 1, 0)
    up = jnp.concatenate([gather_rows(recv, (2 * r, 2 * r + 1), 16) for r in range(2)])
    up = up + norm_back(dy1, gain[1:2, :], unit1, root1)
    unit, root = norm_parts(xin[...])
    y = unit * gain[0:1, :] + shift[0:1, :]
    proj = proj_s[...]
    mixed = mixed_s[...]
    sig = jax.nn.sigmoid(proj[:, 384:512] + gate[0:1, :])
    dgated = dot(up, wout[0], 1, 1)
    dout = dot(sig * mixed, up, 0, 0)
    dmixed = dgated * sig
    dgate = dgated * mixed * sig * (1.0 - sig)
    dproj, dbias = [], 0.0
    for r in range(2):
        part = proj[r * 128 : r * 128 + 128]
        ds, dq, dk, dv = attention_back(
            dmixed[r * 128 : r * 128 + 128],
            part[:, 0:128],
            part[:, 128:256],
            part[:, 256:384],
            probs_s[r * 512 : r * 512 + 512, :],
            False,
        )
        dbias = dbias + ds
        dproj.append(jnp.concatenate([dq, dk, dv, dgate[r * 128 : r * 128 + 128]], axis=1))
    dproj = jnp.concatenate(dproj)
    din = dot(y, dproj, 0, 0)
    dx_o[...] = up + norm_back(dot(dproj, win[0], 1, 1), gain[0:1, :], unit, root)
    for h in range(4):
        scatter_rows(send, (h, 4 + h), 32, dbias[h * 128 : h * 128 + 128])
    for i in range(10):
        source = din[64 * (i % 2) : 64 * (i % 2) + 64, 128 * (i // 2) : 128 * (i // 2) + 128] if i < 8 else dout[64 * (i - 8) : 64 * (i - 8) + 64]
        send[pl.ds(8 + i, 64, stride=32), :] = source
        send[pl.ds(18 + i, 64, stride=32), :] = wgrad[64 * i : 64 * i + 64, :]
    for q in range(64):
        send[q * 32 + 28 : q * 32 + 32, :] = gb1


def fourth_kernel(recv, x, small, shares, totals):
    gain, shift, _, _ = vectors(small)
    total = jnp.sum(recv[...].reshape(64, 32, 128), axis=0)
    unit, root = norm_parts(x[...])
    y = unit * gain[0:1, :] + shift[0:1, :]
    gb0 = dot(total[0:4], y[:128], 1, 0) + dot(total[4:8], y[128:], 1, 0)
    totals[0:8, :] = total[0:8]
    totals[8:16, :] = jnp.concatenate([total[28:32], total[28:32]], axis=0) * (1.0 / 128)
    share = jnp.concatenate([total[8:28], gb0], axis=0) * (1.0 / 128)
    for k in range(4):
        shares[24 * k : 24 * k + 24, :] = share


def tail_kernel(shares, totals, x, dx_s, small, tail):
    gain, _, _, wbias = vectors(small)
    unit, root = norm_parts(x[...])
    dy = jnp.concatenate([dot(totals[4 * r : 4 * r + 4, :], wbias[0], 0, 0) for r in range(2)])
    dx = dx_s[...] + norm_back(dy, gain[0:1, :], unit, root)
    for r in range(2):
        scatter_rows(tail, (r * 128, r * 128 + 1), 2, dx[r * 128 : r * 128 + 128])
    tail[256:352, :] = shares[...]
    tail[352:360, :] = totals[8:16, :]


def last_kernel(recv, gb1, gin, gbias, gout):
    for m in range(2):
        for i in range(10):
            piece = recv[pl.ds(10 * m + i, 64, stride=24), :]
            if i < 8:
                gin[m, 64 * (i % 2) : 64 * (i % 2) + 64, 128 * (i // 2) : 128 * (i // 2) + 128] = piece
            else:
                gout[m, 64 * (i - 8) : 64 * (i - 8) + 64, :] = piece
    gbias[0] = jnp.sum(recv[...].reshape(64, 24, 128), axis=0)[20:24]
    gbias[1] = gb1[0:4]


def call(kernel, outs, *args, cost=None):
    return pl.pallas_call(
        kernel,
        out_shape=tuple(jax.ShapeDtypeStruct(s, f32) for s in outs),
        in_specs=[pl.BlockSpec(memory_space=pltpu.VMEM)] * len(args),
        out_specs=tuple(pl.BlockSpec(memory_space=pltpu.VMEM) for _ in outs),
        cost_estimate=cost,
        compiler_params=pltpu.CompilerParams(vmem_limit_bytes=48 * 1024 * 1024),
    )(*args)


def solution(mesh):
    placed, there, back, fours, planes = plans(mesh)

    def swap(a, groups):
        count = len(groups[0])
        cut = a.reshape(count, a.shape[0] // count, 128)
        got = lax.all_to_all(cut, both, 0, 0, axis_index_groups=groups, tiled=True)
        return got.reshape(a.shape)

    def body(pair, cotangent, gain, shift, win, wb, gate, wout):
        wbias = jnp.transpose(wb, (0, 2, 1)).reshape(8, 128)
        small = jnp.concatenate([gain, shift, gate, jnp.zeros_like(gate), wbias])
        xin = lax.ppermute(pair.reshape(256, 128), both, there)
        cot = lax.ppermute(cotangent.reshape(256, 128), both, there)
        (bsend,) = call(start_kernel, [(512, 128)], xin, small)
        brecv = swap(bsend, placed)
        x, proj, logits = call(
            project_kernel,
            [(256, 128), (256, 512), (1024, 128)],
            *(xin, cot, small, win),
            cost=pl.CostEstimate(flops=10**11, bytes_accessed=4 * 10**8, transcendentals=0),
        )
        send1, probs, mixed, first = call(
            first_kernel,
            [(1024, 128), (1024, 128), (256, 128), (256, 128)],
            *(x, cot, brecv, proj, logits, small, wout),
        )
        recv1 = swap(send1, placed)
        send2, wgrad = call(
            second_kernel, [(1024, 128), (640, 128)], recv1, small, win, wout
        )
        recv2 = swap(send2, placed)
        send3, dx, final = call(
            third_kernel,
            [(2048, 128), (256, 128), (256, 128)],
            *(recv2, x, first, proj, probs, mixed, wgrad, small, win, wout),
        )
        recv3 = swap(send3, placed)
        shares, totals = call(
            fourth_kernel, [(96, 128), (16, 128)], recv3, x, small
        )
        (tail,) = call(
            tail_kernel,
            [(360, 128)],
            *(swap(shares, fours), totals, x, dx, small),
        )
        tail = lax.ppermute(tail, both, back)
        final = lax.ppermute(final, both, back)
        recv4 = swap(
            jnp.broadcast_to(tail[None, 256:352], (16, 96, 128)).reshape(1536, 128), planes
        )
        gin, gbias, gout = call(
            last_kernel, [(2, 128, 512), (2, 4, 128), (2, 128, 128)], recv4, tail[352:360]
        )
        return (
            final.reshape(2, 128, 128),
            tail[0:256].reshape(2, 128, 128),
            gin,
            jnp.transpose(gbias, (0, 2, 1)),
            gout,
        )

    rows = P(("dp", "axial"), None, None)
    part = P("dp", None, None)
    return jax.shard_map(
        body,
        mesh=mesh,
        in_specs=(rows, rows, P(), P(), P(), P(), P(), P()),
        out_specs=(rows, rows, part, part, part),
        check_vma=False,
    )
```

```python
import jax
import jax.numpy as jnp
from jax import lax
from jax.experimental import pallas as pl
from jax.experimental.pallas import tpu as pltpu
from jax.sharding import PartitionSpec as P

f32 = jnp.float32
both = ("dp", "axial")
homes = (
    (5, (2, 0, 1, 3)),
    (7, (2, 3, 0, 1)),
    (1, (0, 2, 3, 1)),
    (3, (0, 1, 2, 3)),
    (6, (2, 0, 1, 3)),
    (0, (2, 3, 0, 1)),
    (4, (0, 1, 2, 3)),
    (2, (0, 2, 3, 1)),
)


def compact_id(part, rank):
    block, places = homes[part]
    place = places[rank % 4]
    z = 2 * block + place // 2
    return ((z % 4) * 2 + place % 2) * 64 + (rank // 4) * 4 + z // 4


def plans(mesh):
    parts, size = mesh.shape["dp"], mesh.shape["axial"]
    if (parts, size) == (8, 64):
        placed = [[compact_id(c, r) for r in range(64)] for c in range(8)]
    else:
        placed = [[c * size + r for r in range(size)] for c in range(parts)]
    there = [(c * size + r, placed[c][r]) for c in range(parts) for r in range(size)]
    back = [(b, a) for a, b in there]
    fours = [ids[4 * b : 4 * b + 4] for ids in placed for b in range(16)]
    planes = [[c * size + 4 * b + k for b in range(16)] for c in range(parts) for k in range(4)]
    return placed, there, back, fours, planes


def dot(a, b, ca, cb):
    return lax.dot_general(
        a, b, (((ca,), (cb,)), ((), ())), precision=lax.Precision.HIGH, preferred_element_type=f32
    )


def norm_parts(x):
    centre = x - jnp.mean(x, axis=-1, keepdims=True)
    root = lax.rsqrt(jnp.mean(centre * centre, axis=-1, keepdims=True) + 1e-05)
    return centre * root, root


def norm_back(dy, gain, unit, root):
    du = dy * gain
    return root * (
        du
        - jnp.mean(du, axis=-1, keepdims=True)
        - unit * jnp.mean(du * unit, axis=-1, keepdims=True)
    )


def by_head(a):
    lane = lax.broadcasted_iota(jnp.int32, a.shape, 1) // 32
    return jnp.concatenate([jnp.where(lane == h, a, 0.0) for h in range(4)], axis=0)


def side_by_side(a):
    return jnp.concatenate([a[128 * h : 128 * h + 128] for h in range(4)], axis=1)


SCALE = 32**-0.5
LONG = pl.CostEstimate(flops=10**11, bytes_accessed=4 * 10**8, transcendentals=0)


def probabilities(q, k, bias, keys_down):
    if keys_down:
        e = jnp.exp(dot(by_head(k), q, 1, 1) * SCALE + bias)
        total = jnp.sum(e.reshape(4, 128, 128), axis=1, keepdims=True)
        return (e.reshape(4, 128, 128) * (1.0 / total)).reshape(512, 128)
    e = jnp.exp(dot(by_head(q), k, 1, 1) * SCALE + bias)
    return e * (1.0 / jnp.sum(e, axis=1, keepdims=True))


def mix(probs, v, keys_down):
    if keys_down:
        return dot(probs, by_head(v), 0, 0)
    return dot(side_by_side(probs), by_head(v), 1, 0)


def attention_back(do, q, k, v, probs, keys_down):
    if keys_down:
        dp = dot(by_head(v), do, 1, 1)
        both_p = (probs * dp).reshape(4, 128, 128)
        ds = (both_p - probs.reshape(4, 128, 128) * jnp.sum(both_p, axis=1, keepdims=True)).reshape(
            512, 128
        )
        dv = dot(side_by_side(probs), by_head(do), 1, 0)
        dk = dot(side_by_side(ds), by_head(q), 1, 0) * SCALE
        dq = dot(ds, by_head(k), 0, 0) * SCALE
    else:
        dp = dot(by_head(do), v, 1, 1)
        both_p = probs * dp
        ds = both_p - probs * jnp.sum(both_p, axis=1, keepdims=True)
        dv = dot(probs, by_head(do), 0, 0)
        dk = dot(ds, by_head(q), 0, 0) * SCALE
        dq = dot(side_by_side(ds), by_head(k), 1, 0) * SCALE
    return ds, dq, dk, dv


def gather_rows(ref, first, stride):
    a, b = first
    return jnp.concatenate([ref[pl.ds(a, 64, stride=stride), :], ref[pl.ds(b, 64, stride=stride), :]])


def scatter_rows(ref, first, stride, value):
    a, b = first
    ref[pl.ds(a, 64, stride=stride), :] = value[:64]
    ref[pl.ds(b, 64, stride=stride), :] = value[64:]


def vectors(small):
    return small[0:2, :], small[2:4, :], small[4:6, :], (small[8:12, :], small[12:16, :])


def start_kernel(xin, small, out):
    gain, shift, _, wbias = vectors(small)
    rows = []
    for r in range(2):
        x = gather_rows(xin, (r * 128, r * 128 + 1), 2)
        unit, root = norm_parts(x)
        rows.append(dot(wbias[0], unit * gain[0:1, :] + shift[0:1, :], 1, 1))
    block = jnp.concatenate(rows, axis=0)
    for q in range(64):
        out[q * 8 : q * 8 + 8, :] = block


def project_kernel(xin, cot, small, win, x_o, proj_o, logits_o):
    gain, shift, _, _ = vectors(small)
    x = jnp.concatenate([gather_rows(xin, (r * 128, r * 128 + 1), 2) for r in range(2)])
    x_o[...] = x
    unit, root = norm_parts(x)
    proj = dot(unit * gain[0:1, :] + shift[0:1, :], win[0], 1, 0)
    proj_o[...] = proj
    for r in range(2):
        part = proj[r * 128 : r * 128 + 128]
        logits_o[r * 512 : r * 512 + 512, :] = (
            dot(by_head(part[:, 0:128]), part[:, 128:256], 1, 1) * SCALE
        )


def first_kernel(x, cot, brecv, proj, logits, small, wout, send, probs_o, mixed_o, first_o):
    gain, shift, gate, wbias = vectors(small)
    bias = jnp.concatenate([gather_rows(brecv, (h, 4 + h), 8) for h in range(4)])
    mixed = []
    for r in range(2):
        e = jnp.exp(logits[r * 512 : r * 512 + 512, :] + bias)
        probs = e * (1.0 / jnp.sum(e, axis=1, keepdims=True))
        probs_o[r * 512 : r * 512 + 512, :] = probs
        mixed.append(mix(probs, proj[r * 128 : r * 128 + 128, 256:384], False))
    mixed = jnp.concatenate(mixed)
    mixed_o[...] = mixed
    gated = jax.nn.sigmoid(proj[:, 384:512] + gate[0:1, :]) * mixed
    first = x[...] + dot(gated, wout[0], 1, 0)
    first_o[...] = first
    unit1, root1 = norm_parts(first)
    y1 = unit1 * gain[1:2, :] + shift[1:2, :]
    bias_rows = jnp.concatenate(
        [dot(wbias[1], y1[r * 128 : r * 128 + 128], 1, 1) for r in range(2)], axis=0
    )
    for q in range(64):
        send[q * 16 + 4 : q * 16 + 12, :] = bias_rows
    for r in range(2):
        scatter_rows(send, (r * 2, r * 2 + 1), 16, first[r * 128 : r * 128 + 128])
        rows = gather_rows(cot, (r * 128, r * 128 + 1), 2)
        scatter_rows(send, (12 + r * 2, 12 + r * 2 + 1), 16, rows)


def second_kernel(recv, small, win, wout, send, wgrad):
    gain, shift, gate, _ = vectors(small)
    bias = jnp.concatenate([gather_rows(recv, (4 + h, 8 + h), 16) for h in range(4)])
    x = jnp.concatenate([gather_rows(recv, (c, 2 + c), 16) for c in range(2)])
    up = jnp.concatenate([gather_rows(recv, (12 + c, 14 + c), 16) for c in range(2)])
    unit, root = norm_parts(x)
    y = unit * gain[1:2, :] + shift[1:2, :]
    proj = dot(y, win[1], 1, 0)
    probs, mixed = [], []
    for c in range(2):
        part = proj[c * 128 : c * 128 + 128]
        probs.append(probabilities(part[:, 0:128], part[:, 128:256], bias, True))
        mixed.append(mix(probs[c], part[:, 256:384], True))
    mixed = jnp.concatenate(mixed)
    sig = jax.nn.sigmoid(proj[:, 384:512] + gate[1:2, :])
    gated = sig * mixed
    final = x + dot(gated, wout[1], 1, 0)
    dgated = dot(up, wout[1], 1, 1)
    dout = dot(gated, up, 0, 0)
    dmixed = dgated * sig
    dgate = dgated * mixed * sig * (1.0 - sig)
    dproj, dbias = [], 0.0
    for c in range(2):
        part = proj[c * 128 : c * 128 + 128]
        ds, dq, dk, dv = attention_back(
            dmixed[c * 128 : c * 128 + 128],
            part[:, 0:128],
            part[:, 128:256],
            part[:, 256:384],
            probs[c],
            True,
        )
        dbias = dbias + ds
        dproj.append(jnp.concatenate([dq, dk, dv, dgate[c * 128 : c * 128 + 128]], axis=1))
    dproj = jnp.concatenate(dproj)
    din = dot(y, dproj, 0, 0)
    dx = up + norm_back(dot(dproj, win[1], 1, 1), gain[1:2, :], unit, root)
    for c in range(2):
        scatter_rows(send, (c, 2 + c), 16, dx[c * 128 : c * 128 + 128])
        scatter_rows(send, (12 + c, 14 + c), 16, final[c * 128 : c * 128 + 128])
    for h in range(4):
        scatter_rows(send, (4 + h, 8 + h), 16, dbias[h * 128 : h * 128 + 128])
    for e in range(4):
        wgrad[e * 128 : e * 128 + 128, :] = din[:, e * 128 : e * 128 + 128]
    wgrad[512:640, :] = dout


def third_kernel(
    recv, xin, first, proj_s, probs_s, mixed_s, wgrad, small, win, wout, send, dx_o, final_o, gb1_o
):
    gain, shift, gate, wbias = vectors(small)
    for r in range(2):
        for c in range(2):
            final_o[pl.ds(r * 128 + c, 64, stride=2), :] = recv[pl.ds(12 + 2 * r + c, 64, stride=16), :]
    summed = jnp.sum(recv[...].reshape(64, 16, 128)[:, 4:12, :], axis=0)
    unit1, root1 = norm_parts(first[...])
    y1 = unit1 * gain[1:2, :] + shift[1:2, :]
    dy1 = jnp.concatenate([dot(summed[4 * r : 4 * r + 4], wbias[1], 0, 0) for r in range(2)])
    gb1 = dot(summed[0:4], y1[:128], 1, 0) + dot(summed[4:8], y1[128:], 1, 0)
    up = jnp.concatenate([gather_rows(recv, (2 * r, 2 * r + 1), 16) for r in range(2)])
    up = up + norm_back(dy1, gain[1:2, :], unit1, root1)
    unit, root = norm_parts(xin[...])
    y = unit * gain[0:1, :] + shift[0:1, :]
    proj = proj_s[...]
    mixed = mixed_s[...]
    sig = jax.nn.sigmoid(proj[:, 384:512] + gate[0:1, :])
    dgated = dot(up, wout[0], 1, 1)
    dout = dot(sig * mixed, up, 0, 0)
    dmixed = dgated * sig
    dgate = dgated * mixed * sig * (1.0 - sig)
    dproj, dbias = [], 0.0
    for r in range(2):
        part = proj[r * 128 : r * 128 + 128]
        ds, dq, dk, dv = attention_back(
            dmixed[r * 128 : r * 128 + 128],
            part[:, 0:128],
            part[:, 128:256],
            part[:, 256:384],
            probs_s[r * 512 : r * 512 + 512, :],
            False,
        )
        dbias = dbias + ds
        dproj.append(jnp.concatenate([dq, dk, dv, dgate[r * 128 : r * 128 + 128]], axis=1))
    dproj = jnp.concatenate(dproj)
    din = dot(y, dproj, 0, 0)
    dx_o[...] = up + norm_back(dot(dproj, win[0], 1, 1), gain[0:1, :], unit, root)
    for h in range(4):
        scatter_rows(send, (h, 4 + h), 28, dbias[h * 128 : h * 128 + 128])
    for i in range(10):
        source = din[64 * (i % 2) : 64 * (i % 2) + 64, 128 * (i // 2) : 128 * (i // 2) + 128] if i < 8 else dout[64 * (i - 8) : 64 * (i - 8) + 64]
        send[pl.ds(8 + i, 64, stride=28), :] = source
        send[pl.ds(18 + i, 64, stride=28), :] = wgrad[64 * i : 64 * i + 64, :]
    gb1_o[0:4, :] = gb1
    gb1_o[4:8, :] = gb1


def fourth_kernel(recv, x, gb1, small, shares, totals):
    gain, shift, _, _ = vectors(small)
    pair_sum = jnp.sum(recv[...].reshape(32, 56, 128), axis=0)
    total = pair_sum[0:28] + pair_sum[28:56]
    unit, root = norm_parts(x[...])
    y = unit * gain[0:1, :] + shift[0:1, :]
    gb0 = dot(total[0:4], y[:128], 1, 0) + dot(total[4:8], y[128:], 1, 0)
    totals[...] = total[0:8]
    share = jnp.concatenate([total[8:28], gb0, gb1[0:4, :], jnp.zeros((4, 128), f32)], axis=0) * (1.0 / 128)
    for k in range(4):
        shares[32 * k : 32 * k + 32, :] = share


def tail_kernel(shares, totals, x, dx_s, small, tail):
    gain, _, _, wbias = vectors(small)
    unit, root = norm_parts(x[...])
    dy = jnp.concatenate([dot(totals[4 * r : 4 * r + 4, :], wbias[0], 0, 0) for r in range(2)])
    dx = dx_s[...] + norm_back(dy, gain[0:1, :], unit, root)
    for r in range(2):
        scatter_rows(tail, (r * 128, r * 128 + 1), 2, dx[r * 128 : r * 128 + 128])
    for k in range(4):
        tail[256 + 20 * k : 276 + 20 * k, :] = shares[32 * k : 32 * k + 20, :]
    tail[336:344, :] = jnp.sum(shares[...].reshape(4, 32, 128)[:, 20:28, :], axis=0)


def last_kernel(recv, tail, final, gin, gbias, gout, grad_o, final_o, rows):
    for j in range(20):
        for k in range(4):
            rows[pl.ds(64 * j + k, 16, stride=4), :] = recv[pl.ds(20 * k + j, 16, stride=88), :]
    for m in range(2):
        for e in range(4):
            first = 640 * m + 128 * e
            gin[m, :, 128 * e : 128 * e + 128] = rows[first : first + 128, :]
        gout[m] = rows[640 * m + 512 : 640 * m + 640, :]
    both_bias = jnp.sum(recv[...].reshape(16, 88, 128), axis=0)[80:88]
    gbias[0] = both_bias[0:4]
    gbias[1] = both_bias[4:8]
    grad_o[...] = tail[0:256, :]
    final_o[...] = final[...]


def call(kernel, outs, *args, cost=None, scratch=()):
    return pl.pallas_call(
        kernel,
        out_shape=tuple(jax.ShapeDtypeStruct(s, f32) for s in outs),
        in_specs=[pl.BlockSpec(memory_space=pltpu.VMEM)] * len(args),
        out_specs=tuple(pl.BlockSpec(memory_space=pltpu.VMEM) for _ in outs),
        scratch_shapes=scratch,
        cost_estimate=cost,
        compiler_params=pltpu.CompilerParams(vmem_limit_bytes=48 * 1024 * 1024),
    )(*args)


def solution(mesh):
    placed, there, back, fours, planes = plans(mesh)

    def swap(a, groups):
        each = a.shape[0] // len(groups[0])
        tile = 8 if each % 8 == 0 else 4
        cut = a.reshape(a.shape[0] // tile, tile, 128) if tile == 4 else a.reshape(-1, each, 128)
        got = lax.all_to_all(cut, both, 0, 0, axis_index_groups=groups, tiled=True)
        return got.reshape(a.shape)

    def body(pair, cotangent, gain, shift, win, wb, gate, wout):
        wbias = jnp.transpose(wb, (0, 2, 1)).reshape(8, 128)
        small = jnp.concatenate([gain, shift, gate, jnp.zeros_like(gate), wbias])
        xin = lax.ppermute(pair.reshape(256, 128), both, there)
        cot = lax.ppermute(cotangent.reshape(256, 128), both, there)
        (bsend,) = call(start_kernel, [(512, 128)], xin, small)
        brecv = swap(bsend, placed)
        x, proj, logits = call(
            project_kernel,
            [(256, 128), (256, 512), (1024, 128)],
            *(xin, cot, small, win),
            cost=LONG,
        )
        send1, probs, mixed, first = call(
            first_kernel,
            [(1024, 128), (1024, 128), (256, 128), (256, 128)],
            *(x, cot, brecv, proj, logits, small, wout),
        )
        recv1 = swap(send1, placed)
        send2, wgrad = call(
            second_kernel, [(1024, 128), (640, 128)], recv1, small, win, wout
        )
        recv2 = swap(send2, placed)
        send3, dx, final, gb1 = call(
            third_kernel,
            [(1792, 128), (256, 128), (256, 128), (8, 128)],
            *(recv2, x, first, proj, probs, mixed, wgrad, small, win, wout),
        )
        recv3 = swap(send3, placed)
        shares, totals = call(
            fourth_kernel, [(128, 128), (8, 128)], recv3, x, gb1, small
        )
        (tail,) = call(
            tail_kernel,
            [(344, 128)],
            *(swap(shares, fours), totals, x, dx, small),
        )
        tail = lax.ppermute(tail, both, back)
        final = lax.ppermute(final, both, back)
        recv4 = swap(
            jnp.broadcast_to(tail[None, 256:344], (16, 88, 128)).reshape(1408, 128), planes
        )
        gin, gbias, gout, grad, final = call(
            last_kernel,
            [(2, 128, 512), (2, 4, 128), (2, 128, 128), (256, 128), (256, 128)],
            *(recv4, tail, final),
            scratch=[pltpu.VMEM((1280, 128), f32)],
        )
        return (
            final.reshape(2, 128, 128),
            grad.reshape(2, 128, 128),
            gin,
            jnp.transpose(gbias, (0, 2, 1)),
            gout,
        )

    rows = P(("dp", "axial"), None, None)
    part = P("dp", None, None)
    return jax.shard_map(
        body,
        mesh=mesh,
        in_specs=(rows, rows, P(), P(), P(), P(), P(), P()),
        out_specs=(rows, rows, part, part, part),
        check_vma=False,
    )
```

```python
import jax
import jax.numpy as jnp
from jax import lax
from jax.experimental import pallas as pl
from jax.experimental.pallas import tpu as pltpu
from jax.sharding import PartitionSpec as P

f32 = jnp.float32
both = ("dp", "axial")
homes = (
    (5, (2, 0, 1, 3)),
    (7, (2, 3, 0, 1)),
    (1, (0, 2, 3, 1)),
    (3, (0, 1, 2, 3)),
    (6, (2, 0, 1, 3)),
    (0, (2, 3, 0, 1)),
    (4, (0, 1, 2, 3)),
    (2, (0, 2, 3, 1)),
)


def compact_id(part, rank):
    block, places = homes[part]
    place = places[rank % 4]
    z = 2 * block + place // 2
    return ((z % 4) * 2 + place % 2) * 64 + (rank // 4) * 4 + z // 4


def plans(mesh):
    parts, size = mesh.shape["dp"], mesh.shape["axial"]
    if (parts, size) == (8, 64):
        placed = [[compact_id(c, r) for r in range(64)] for c in range(8)]
    else:
        placed = [[c * size + r for r in range(size)] for c in range(parts)]
    there = [(c * size + r, placed[c][r]) for c in range(parts) for r in range(size)]
    back = [(b, a) for a, b in there]
    fours = [ids[4 * b : 4 * b + 4] for ids in placed for b in range(16)]
    planes = [[c * size + 4 * b + k for b in range(16)] for c in range(parts) for k in range(4)]
    return placed, there, back, fours, planes


def halves(a):
    if isinstance(a, tuple):
        return a
    high = a.astype(jnp.bfloat16)
    return high, (a - high.astype(f32)).astype(jnp.bfloat16)


def product(a, b, ca, cb):
    return lax.dot_general(a, b, (((ca,), (cb,)), ((), ())), preferred_element_type=f32)


def dot(a, b, ca, cb):
    (ah, al), (bh, bl) = halves(a), halves(b)
    n = bh.shape[1 - cb]
    if ca == 0:
        if n > 128:
            return product(ah, bh, 0, 0) + (product(ah, bl, 0, 0) + product(al, bh, 0, 0))
        r = product(ah, jnp.concatenate([bh, bl], axis=1), 0, 0)
        return r[:, :n] + (r[:, n:] + product(al, bh, 0, 0))
    deep = jnp.concatenate([ah, al], axis=1)
    if n != 128 or ah.shape[1] != 128:
        return product(deep, jnp.concatenate([bh, bh], axis=cb), 1, cb) + product(ah, bl, 1, cb)
    highs = jnp.concatenate([bh, bh], axis=cb)
    lows = jnp.concatenate([bl, jnp.zeros_like(bl)], axis=cb)
    r = product(deep, jnp.concatenate([highs, lows], axis=1 - cb), 1, cb)
    return r[:, :n] + r[:, n:]


def norm_parts(x):
    centre = x - jnp.mean(x, axis=-1, keepdims=True)
    root = lax.rsqrt(jnp.mean(centre * centre, axis=-1, keepdims=True) + 1e-05)
    return centre * root, root


def norm_back(dy, gain, unit, root):
    du = dy * gain
    return root * (
        du
        - jnp.mean(du, axis=-1, keepdims=True)
        - unit * jnp.mean(du * unit, axis=-1, keepdims=True)
    )


def by_head(a):
    if isinstance(a, tuple):
        return tuple(by_head(part) for part in a)
    lane = lax.broadcasted_iota(jnp.int32, (1, 128), 1) // 32
    return jnp.concatenate([a * (lane == h).astype(a.dtype) for h in range(4)], axis=0)


def side_by_side(a):
    if isinstance(a, tuple):
        return tuple(side_by_side(part) for part in a)
    return jnp.concatenate([a[128 * h : 128 * h + 128] for h in range(4)], axis=1)


SCALE = 32**-0.5
LONG = pl.CostEstimate(flops=10**11, bytes_accessed=4 * 10**8, transcendentals=0)


def probabilities(q, k, bias, keys_down):
    if keys_down:
        e = jnp.exp(dot(by_head(halves(k)), q, 1, 1) * SCALE + bias).reshape(4, 128, 128)
        return (e * (1.0 / jnp.sum(e, axis=1, keepdims=True))).reshape(512, 128)
    e = jnp.exp(dot(by_head(halves(q)), k, 1, 1) * SCALE + bias)
    return e * (1.0 / jnp.sum(e, axis=1, keepdims=True))


def mix(probs, v, keys_down):
    if keys_down:
        return dot(probs, by_head(halves(v)), 0, 0)
    return dot(side_by_side(halves(probs)), by_head(halves(v)), 1, 0)


def attention_back(do, q, k, v, probs, keys_down):
    do, q, k, v = halves(do), halves(q), halves(k), halves(v)
    split_probs = halves(probs)
    if keys_down:
        dp = dot(by_head(v), do, 1, 1)
        both_p = (probs * dp).reshape(4, 128, 128)
        ds = (both_p - probs.reshape(4, 128, 128) * jnp.sum(both_p, axis=1, keepdims=True)).reshape(
            512, 128
        )
        dv = dot(side_by_side(split_probs), by_head(do), 1, 0)
        split_ds = halves(ds)
        dk = dot(side_by_side(split_ds), by_head(q), 1, 0) * SCALE
        dq = dot(split_ds, by_head(k), 0, 0) * SCALE
    else:
        dp = dot(by_head(do), v, 1, 1)
        both_p = probs * dp
        ds = both_p - probs * jnp.sum(both_p, axis=1, keepdims=True)
        dv = dot(split_probs, by_head(do), 0, 0)
        split_ds = halves(ds)
        dk = dot(split_ds, by_head(q), 0, 0) * SCALE
        dq = dot(side_by_side(split_ds), by_head(k), 1, 0) * SCALE
    return ds, dq, dk, dv


def gather_rows(ref, first, stride):
    a, b = first
    return jnp.concatenate([ref[pl.ds(a, 64, stride=stride), :], ref[pl.ds(b, 64, stride=stride), :]])


def scatter_rows(ref, first, stride, value):
    a, b = first
    ref[pl.ds(a, 64, stride=stride), :] = value[:64]
    ref[pl.ds(b, 64, stride=stride), :] = value[64:]


def vectors(small):
    return small[0:2, :], small[2:4, :], small[4:6, :], (small[8:12, :], small[12:16, :])


def start_kernel(xin, small, out):
    gain, shift, _, wbias = vectors(small)
    rows = []
    for r in range(2):
        x = gather_rows(xin, (r * 128, r * 128 + 1), 2)
        unit, root = norm_parts(x)
        rows.append(dot(wbias[0], unit * gain[0:1, :] + shift[0:1, :], 1, 1))
    block = jnp.concatenate(rows, axis=0)
    for q in range(64):
        out[q * 8 : q * 8 + 8, :] = block


def project_kernel(xin, cot, small, win, x_o, proj_o, logits_o):
    gain, shift, _, _ = vectors(small)
    x = jnp.concatenate([gather_rows(xin, (r * 128, r * 128 + 1), 2) for r in range(2)])
    x_o[...] = x
    unit, root = norm_parts(x)
    proj = dot(unit * gain[0:1, :] + shift[0:1, :], win[0], 1, 0)
    proj_o[...] = proj
    for r in range(2):
        part = proj[r * 128 : r * 128 + 128]
        logits_o[r * 512 : r * 512 + 512, :] = (
            dot(by_head(halves(part[:, 0:128])), part[:, 128:256], 1, 1) * SCALE
        )


def first_kernel(x, cot, brecv, proj, logits, small, wout, send, probs_o, mixed_o, first_o):
    gain, shift, gate, wbias = vectors(small)
    bias = jnp.concatenate([gather_rows(brecv, (h, 4 + h), 8) for h in range(4)])
    mixed = []
    for r in range(2):
        e = jnp.exp(logits[r * 512 : r * 512 + 512, :] + bias)
        probs = e * (1.0 / jnp.sum(e, axis=1, keepdims=True))
        probs_o[r * 512 : r * 512 + 512, :] = probs
        mixed.append(mix(probs, proj[r * 128 : r * 128 + 128, 256:384], False))
    mixed = jnp.concatenate(mixed)
    mixed_o[...] = mixed
    gated = jax.nn.sigmoid(proj[:, 384:512] + gate[0:1, :]) * mixed
    first = x[...] + dot(gated, wout[0], 1, 0)
    first_o[...] = first
    unit1, root1 = norm_parts(first)
    y1 = unit1 * gain[1:2, :] + shift[1:2, :]
    bias_rows = jnp.concatenate(
        [dot(wbias[1], y1[r * 128 : r * 128 + 128], 1, 1) for r in range(2)], axis=0
    )
    for q in range(64):
        send[q * 16 + 4 : q * 16 + 12, :] = bias_rows
    for r in range(2):
        scatter_rows(send, (r * 2, r * 2 + 1), 16, first[r * 128 : r * 128 + 128])
        rows = gather_rows(cot, (r * 128, r * 128 + 1), 2)
        scatter_rows(send, (12 + r * 2, 12 + r * 2 + 1), 16, rows)


def second_kernel(recv, small, win, wout, send, wgrad):
    gain, shift, gate, _ = vectors(small)
    bias = jnp.concatenate([gather_rows(recv, (4 + h, 8 + h), 16) for h in range(4)])
    x = jnp.concatenate([gather_rows(recv, (c, 2 + c), 16) for c in range(2)])
    up = jnp.concatenate([gather_rows(recv, (12 + c, 14 + c), 16) for c in range(2)])
    unit, root = norm_parts(x)
    y = unit * gain[1:2, :] + shift[1:2, :]
    proj = dot(y, win[1], 1, 0)
    probs, mixed = [], []
    for c in range(2):
        part = proj[c * 128 : c * 128 + 128]
        probs.append(probabilities(part[:, 0:128], part[:, 128:256], bias, True))
        mixed.append(mix(probs[c], part[:, 256:384], True))
    mixed = jnp.concatenate(mixed)
    sig = jax.nn.sigmoid(proj[:, 384:512] + gate[1:2, :])
    gated = sig * mixed
    final = x + dot(gated, wout[1], 1, 0)
    dgated = dot(up, wout[1], 1, 1)
    dout = dot(gated, up, 0, 0)
    dmixed = dgated * sig
    dgate = dgated * mixed * sig * (1.0 - sig)
    dproj, dbias = [], 0.0
    for c in range(2):
        part = proj[c * 128 : c * 128 + 128]
        ds, dq, dk, dv = attention_back(
            dmixed[c * 128 : c * 128 + 128],
            part[:, 0:128],
            part[:, 128:256],
            part[:, 256:384],
            probs[c],
            True,
        )
        dbias = dbias + ds
        dproj.append(jnp.concatenate([dq, dk, dv, dgate[c * 128 : c * 128 + 128]], axis=1))
    dproj = jnp.concatenate(dproj)
    din = dot(y, dproj, 0, 0)
    dx = up + norm_back(dot(dproj, win[1], 1, 1), gain[1:2, :], unit, root)
    for c in range(2):
        scatter_rows(send, (c, 2 + c), 16, dx[c * 128 : c * 128 + 128])
        scatter_rows(send, (12 + c, 14 + c), 16, final[c * 128 : c * 128 + 128])
    for h in range(4):
        scatter_rows(send, (4 + h, 8 + h), 16, dbias[h * 128 : h * 128 + 128])
    for e in range(4):
        wgrad[e * 128 : e * 128 + 128, :] = din[:, e * 128 : e * 128 + 128]
    wgrad[512:640, :] = dout


def third_kernel(
    recv, xin, first, proj_s, probs_s, mixed_s, wgrad, small, win, wout, send, dx_o, final_o, gb1_o
):
    gain, shift, gate, wbias = vectors(small)
    for r in range(2):
        for c in range(2):
            final_o[pl.ds(r * 128 + c, 64, stride=2), :] = recv[pl.ds(12 + 2 * r + c, 64, stride=16), :]
    summed = jnp.sum(recv[...].reshape(64, 16, 128)[:, 4:12, :], axis=0)
    unit1, root1 = norm_parts(first[...])
    y1 = unit1 * gain[1:2, :] + shift[1:2, :]
    dy1 = jnp.concatenate([dot(summed[4 * r : 4 * r + 4], wbias[1], 0, 0) for r in range(2)])
    gb1 = dot(summed[0:4], y1[:128], 1, 0) + dot(summed[4:8], y1[128:], 1, 0)
    up = jnp.concatenate([gather_rows(recv, (2 * r, 2 * r + 1), 16) for r in range(2)])
    up = up + norm_back(dy1, gain[1:2, :], unit1, root1)
    unit, root = norm_parts(xin[...])
    y = unit * gain[0:1, :] + shift[0:1, :]
    proj = proj_s[...]
    mixed = mixed_s[...]
    sig = jax.nn.sigmoid(proj[:, 384:512] + gate[0:1, :])
    dgated = dot(up, wout[0], 1, 1)
    dout = dot(sig * mixed, up, 0, 0)
    dmixed = dgated * sig
    dgate = dgated * mixed * sig * (1.0 - sig)
    dproj, dbias = [], 0.0
    for r in range(2):
        part = proj[r * 128 : r * 128 + 128]
        ds, dq, dk, dv = attention_back(
            dmixed[r * 128 : r * 128 + 128],
            part[:, 0:128],
            part[:, 128:256],
            part[:, 256:384],
            probs_s[r * 512 : r * 512 + 512, :],
            False,
        )
        dbias = dbias + ds
        dproj.append(jnp.concatenate([dq, dk, dv, dgate[r * 128 : r * 128 + 128]], axis=1))
    dproj = jnp.concatenate(dproj)
    din = dot(y, dproj, 0, 0)
    dx_o[...] = up + norm_back(dot(dproj, win[0], 1, 1), gain[0:1, :], unit, root)
    for h in range(4):
        scatter_rows(send, (h, 4 + h), 28, dbias[h * 128 : h * 128 + 128])
    for i in range(10):
        source = din[64 * (i % 2) : 64 * (i % 2) + 64, 128 * (i // 2) : 128 * (i // 2) + 128] if i < 8 else dout[64 * (i - 8) : 64 * (i - 8) + 64]
        send[pl.ds(8 + i, 64, stride=28), :] = source
        send[pl.ds(18 + i, 64, stride=28), :] = wgrad[64 * i : 64 * i + 64, :]
    gb1_o[0:4, :] = gb1
    gb1_o[4:8, :] = gb1


def fourth_kernel(recv, x, gb1, small, shares, totals):
    gain, shift, _, _ = vectors(small)
    pair_sum = jnp.sum(recv[...].reshape(32, 56, 128), axis=0)
    total = pair_sum[0:28] + pair_sum[28:56]
    unit, root = norm_parts(x[...])
    y = unit * gain[0:1, :] + shift[0:1, :]
    gb0 = dot(total[0:4], y[:128], 1, 0) + dot(total[4:8], y[128:], 1, 0)
    totals[...] = total[0:8]
    share = jnp.concatenate([total[8:28], gb0, gb1[0:4, :], jnp.zeros((4, 128), f32)], axis=0) * (1.0 / 128)
    for k in range(4):
        shares[32 * k : 32 * k + 32, :] = share


def tail_kernel(shares, totals, x, dx_s, small, tail):
    gain, _, _, wbias = vectors(small)
    unit, root = norm_parts(x[...])
    dy = jnp.concatenate([dot(totals[4 * r : 4 * r + 4, :], wbias[0], 0, 0) for r in range(2)])
    dx = dx_s[...] + norm_back(dy, gain[0:1, :], unit, root)
    for r in range(2):
        scatter_rows(tail, (r * 128, r * 128 + 1), 2, dx[r * 128 : r * 128 + 128])
    for k in range(4):
        tail[256 + 20 * k : 276 + 20 * k, :] = shares[32 * k : 32 * k + 20, :]
    tail[336:344, :] = jnp.sum(shares[...].reshape(4, 32, 128)[:, 20:28, :], axis=0)


def emit_kernel(tail, final, grad_o, final_o, mark):
    grad_o[...] = tail[0:256, :]
    final_o[...] = final[...]
    mark[...] = tail[336:344, :]


def last_kernel(recv, mark, gin, gbias, gout, rows):
    for j in range(20):
        for k in range(4):
            rows[pl.ds(64 * j + k, 16, stride=4), :] = recv[pl.ds(20 * k + j, 16, stride=88), :]
    for m in range(2):
        for e in range(4):
            first = 640 * m + 128 * e
            gin[m, :, 128 * e : 128 * e + 128] = rows[first : first + 128, :]
        gout[m] = rows[640 * m + 512 : 640 * m + 640, :]
    both_bias = jnp.sum(recv[...].reshape(16, 88, 128), axis=0)[80:88]
    gbias[0] = both_bias[0:4]
    gbias[1] = both_bias[4:8]


def call(kernel, outs, *args, cost=None, scratch=()):
    return pl.pallas_call(
        kernel,
        out_shape=tuple(jax.ShapeDtypeStruct(s, f32) for s in outs),
        in_specs=[pl.BlockSpec(memory_space=pltpu.VMEM)] * len(args),
        out_specs=tuple(pl.BlockSpec(memory_space=pltpu.VMEM) for _ in outs),
        scratch_shapes=scratch,
        cost_estimate=cost,
        compiler_params=pltpu.CompilerParams(vmem_limit_bytes=48 * 1024 * 1024),
    )(*args)


def solution(mesh):
    placed, there, back, fours, planes = plans(mesh)

    def swap(a, groups):
        each = a.shape[0] // len(groups[0])
        tile = 8 if each % 8 == 0 else 4
        cut = a.reshape(a.shape[0] // tile, tile, 128) if tile == 4 else a.reshape(-1, each, 128)
        got = lax.all_to_all(cut, both, 0, 0, axis_index_groups=groups, tiled=True)
        return got.reshape(a.shape)

    def body(pair, cotangent, gain, shift, win, wb, gate, wout):
        wbias = jnp.transpose(wb, (0, 2, 1)).reshape(8, 128)
        small = jnp.concatenate([gain, shift, gate, jnp.zeros_like(gate), wbias])
        xin = lax.ppermute(pair.reshape(256, 128), both, there)
        cot = lax.ppermute(cotangent.reshape(256, 128), both, there)
        (bsend,) = call(start_kernel, [(512, 128)], xin, small)
        brecv = swap(bsend, placed)
        x, proj, logits = call(
            project_kernel,
            [(256, 128), (256, 512), (1024, 128)],
            *(xin, cot, small, win),
            cost=LONG,
        )
        send1, probs, mixed, first = call(
            first_kernel,
            [(1024, 128), (1024, 128), (256, 128), (256, 128)],
            *(x, cot, brecv, proj, logits, small, wout),
        )
        recv1 = swap(send1, placed)
        send2, wgrad = call(
            second_kernel, [(1024, 128), (640, 128)], recv1, small, win, wout
        )
        recv2 = swap(send2, placed)
        send3, dx, final, gb1 = call(
            third_kernel,
            [(1792, 128), (256, 128), (256, 128), (8, 128)],
            *(recv2, x, first, proj, probs, mixed, wgrad, small, win, wout),
        )
        recv3 = swap(send3, placed)
        shares, totals = call(
            fourth_kernel, [(128, 128), (8, 128)], recv3, x, gb1, small
        )
        (tail,) = call(
            tail_kernel,
            [(344, 128)],
            *(swap(shares, fours), totals, x, dx, small),
        )
        tail = lax.ppermute(tail, both, back)
        final = lax.ppermute(final, both, back)
        recv4 = swap(
            jnp.broadcast_to(tail[None, 256:344], (16, 88, 128)).reshape(1408, 128), planes
        )
        grad, final, mark = call(
            emit_kernel, [(256, 128), (256, 128), (8, 128)], tail, final, cost=LONG
        )
        gin, gbias, gout = call(
            last_kernel,
            [(2, 128, 512), (2, 4, 128), (2, 128, 128)],
            *(recv4, mark),
            scratch=[pltpu.VMEM((1280, 128), f32)],
        )
        return (
            final.reshape(2, 128, 128),
            grad.reshape(2, 128, 128),
            gin,
            jnp.transpose(gbias, (0, 2, 1)),
            gout,
        )

    rows = P(("dp", "axial"), None, None)
    part = P("dp", None, None)
    return jax.shard_map(
        body,
        mesh=mesh,
        in_specs=(rows, rows, P(), P(), P(), P(), P(), P()),
        out_specs=(rows, rows, part, part, part),
        check_vma=False,
    )
```

```python
import jax
import jax.numpy as jnp
from jax import lax
from jax.experimental import pallas as pl
from jax.experimental.pallas import tpu as pltpu
from jax.sharding import PartitionSpec as P

f32 = jnp.float32
both = ("dp", "axial")
homes = (
    (5, (2, 0, 1, 3)),
    (7, (2, 3, 0, 1)),
    (1, (0, 2, 3, 1)),
    (3, (0, 1, 2, 3)),
    (6, (2, 0, 1, 3)),
    (0, (2, 3, 0, 1)),
    (4, (0, 1, 2, 3)),
    (2, (0, 2, 3, 1)),
)


def compact_id(part, rank):
    block, places = homes[part]
    place = places[rank % 4]
    z = 2 * block + place // 2
    return ((z % 4) * 2 + place % 2) * 64 + (rank // 4) * 4 + z // 4


def plans(mesh):
    parts, size = mesh.shape["dp"], mesh.shape["axial"]
    if (parts, size) == (8, 64):
        placed = [[compact_id(c, r) for r in range(64)] for c in range(8)]
    else:
        placed = [[c * size + r for r in range(size)] for c in range(parts)]
    there = [(c * size + r, placed[c][r]) for c in range(parts) for r in range(size)]
    back = [(b, a) for a, b in there]
    fours = [ids[4 * b : 4 * b + 4] for ids in placed for b in range(16)]
    planes = [[c * size + 4 * b + k for b in range(16)] for c in range(parts) for k in range(4)]
    return placed, there, back, fours, planes


def halves(a):
    if isinstance(a, tuple):
        return a
    high = a.astype(jnp.bfloat16)
    return high, (a - high.astype(f32)).astype(jnp.bfloat16)


def product(a, b, ca, cb):
    return lax.dot_general(a, b, (((ca,), (cb,)), ((), ())), preferred_element_type=f32)


def dot(a, b, ca, cb):
    (ah, al), (bh, bl) = halves(a), halves(b)
    n = bh.shape[1 - cb]
    if ca == 0:
        if n > 128:
            return product(ah, bh, 0, 0) + (product(ah, bl, 0, 0) + product(al, bh, 0, 0))
        r = product(ah, jnp.concatenate([bh, bl], axis=1), 0, 0)
        return r[:, :n] + (r[:, n:] + product(al, bh, 0, 0))
    deep = jnp.concatenate([ah, al], axis=1)
    if n != 128 or ah.shape[1] != 128:
        return product(deep, jnp.concatenate([bh, bh], axis=cb), 1, cb) + product(ah, bl, 1, cb)
    highs = jnp.concatenate([bh, bh], axis=cb)
    lows = jnp.concatenate([bl, jnp.zeros_like(bl)], axis=cb)
    r = product(deep, jnp.concatenate([highs, lows], axis=1 - cb), 1, cb)
    return r[:, :n] + r[:, n:]


def norm_parts(x):
    centre = x - jnp.mean(x, axis=-1, keepdims=True)
    root = lax.rsqrt(jnp.mean(centre * centre, axis=-1, keepdims=True) + 1e-05)
    return centre * root, root


def norm_back(dy, gain, unit, root):
    du = dy * gain
    return root * (
        du
        - jnp.mean(du, axis=-1, keepdims=True)
        - unit * jnp.mean(du * unit, axis=-1, keepdims=True)
    )


def by_head(a):
    if isinstance(a, tuple):
        return tuple(by_head(part) for part in a)
    lane = lax.broadcasted_iota(jnp.int32, (1, 128), 1) // 32
    return jnp.concatenate([a * (lane == h).astype(a.dtype) for h in range(4)], axis=0)


def side_by_side(a):
    if isinstance(a, tuple):
        return tuple(side_by_side(part) for part in a)
    return jnp.concatenate([a[128 * h : 128 * h + 128] for h in range(4)], axis=1)


SCALE = 32**-0.5
LONG = pl.CostEstimate(flops=10**11, bytes_accessed=4 * 10**8, transcendentals=0)


def probabilities(q, k, bias, keys_down):
    if keys_down:
        e = jnp.exp(dot(by_head(halves(k)), q, 1, 1) * SCALE + bias).reshape(4, 128, 128)
        return (e * (1.0 / jnp.sum(e, axis=1, keepdims=True))).reshape(512, 128)
    e = jnp.exp(dot(by_head(halves(q)), k, 1, 1) * SCALE + bias)
    return e * (1.0 / jnp.sum(e, axis=1, keepdims=True))


def mix(probs, v, keys_down):
    if keys_down:
        return dot(probs, by_head(halves(v)), 0, 0)
    return dot(side_by_side(halves(probs)), by_head(halves(v)), 1, 0)


def attention_back(do, q, k, v, probs, keys_down):
    do, q, k, v = halves(do), halves(q), halves(k), halves(v)
    split_probs = halves(probs)
    if keys_down:
        dp = dot(by_head(v), do, 1, 1)
        both_p = (probs * dp).reshape(4, 128, 128)
        ds = (both_p - probs.reshape(4, 128, 128) * jnp.sum(both_p, axis=1, keepdims=True)).reshape(
            512, 128
        )
        dv = dot(side_by_side(split_probs), by_head(do), 1, 0)
        split_ds = halves(ds)
        dk = dot(side_by_side(split_ds), by_head(q), 1, 0) * SCALE
        dq = dot(split_ds, by_head(k), 0, 0) * SCALE
    else:
        dp = dot(by_head(do), v, 1, 1)
        both_p = probs * dp
        ds = both_p - probs * jnp.sum(both_p, axis=1, keepdims=True)
        dv = dot(split_probs, by_head(do), 0, 0)
        split_ds = halves(ds)
        dk = dot(split_ds, by_head(q), 0, 0) * SCALE
        dq = dot(side_by_side(split_ds), by_head(k), 1, 0) * SCALE
    return ds, dq, dk, dv


def gather_rows(ref, first, stride):
    a, b = first
    return jnp.concatenate([ref[pl.ds(a, 64, stride=stride), :], ref[pl.ds(b, 64, stride=stride), :]])


def scatter_rows(ref, first, stride, value):
    a, b = first
    ref[pl.ds(a, 64, stride=stride), :] = value[:64]
    ref[pl.ds(b, 64, stride=stride), :] = value[64:]


def vectors(small):
    return small[0:2, :], small[2:4, :], small[4:6, :], (small[8:12, :], small[12:16, :])


def start_kernel(xin, small, out):
    gain, shift, _, wbias = vectors(small)
    rows = []
    for r in range(2):
        x = gather_rows(xin, (r * 128, r * 128 + 1), 2)
        unit, root = norm_parts(x)
        rows.append(dot(wbias[0], unit * gain[0:1, :] + shift[0:1, :], 1, 1))
    block = jnp.concatenate(rows, axis=0)
    for q in range(64):
        out[q * 8 : q * 8 + 8, :] = block


def project_kernel(xin, cot, small, win, x_o, proj_o, logits_o):
    gain, shift, _, _ = vectors(small)
    x = jnp.concatenate([gather_rows(xin, (r * 128, r * 128 + 1), 2) for r in range(2)])
    x_o[...] = x
    unit, root = norm_parts(x)
    proj = dot(unit * gain[0:1, :] + shift[0:1, :], win[0], 1, 0)
    proj_o[...] = proj
    for r in range(2):
        part = proj[r * 128 : r * 128 + 128]
        logits_o[r * 512 : r * 512 + 512, :] = (
            dot(by_head(halves(part[:, 0:128])), part[:, 128:256], 1, 1) * SCALE
        )


def first_kernel(x, cot, brecv, proj, logits, small, wout, send, probs_o, mixed_o, first_o):
    gain, shift, gate, wbias = vectors(small)
    bias = jnp.concatenate([gather_rows(brecv, (h, 4 + h), 8) for h in range(4)])
    mixed = []
    for r in range(2):
        e = jnp.exp(logits[r * 512 : r * 512 + 512, :] + bias)
        probs = e * (1.0 / jnp.sum(e, axis=1, keepdims=True))
        probs_o[r * 512 : r * 512 + 512, :] = probs
        mixed.append(mix(probs, proj[r * 128 : r * 128 + 128, 256:384], False))
    mixed = jnp.concatenate(mixed)
    mixed_o[...] = mixed
    gated = jax.nn.sigmoid(proj[:, 384:512] + gate[0:1, :]) * mixed
    first = x[...] + dot(gated, wout[0], 1, 0)
    first_o[...] = first
    unit1, root1 = norm_parts(first)
    y1 = unit1 * gain[1:2, :] + shift[1:2, :]
    bias_rows = jnp.concatenate(
        [dot(wbias[1], y1[r * 128 : r * 128 + 128], 1, 1) for r in range(2)], axis=0
    )
    for q in range(64):
        send[q * 16 + 4 : q * 16 + 12, :] = bias_rows
    for r in range(2):
        scatter_rows(send, (r * 2, r * 2 + 1), 16, first[r * 128 : r * 128 + 128])
        rows = gather_rows(cot, (r * 128, r * 128 + 1), 2)
        scatter_rows(send, (12 + r * 2, 12 + r * 2 + 1), 16, rows)


def second_kernel(recv, small, win, wout, send, wgrad):
    gain, shift, gate, _ = vectors(small)
    bias = jnp.concatenate([gather_rows(recv, (4 + h, 8 + h), 16) for h in range(4)])
    x = jnp.concatenate([gather_rows(recv, (c, 2 + c), 16) for c in range(2)])
    up = jnp.concatenate([gather_rows(recv, (12 + c, 14 + c), 16) for c in range(2)])
    unit, root = norm_parts(x)
    y = unit * gain[1:2, :] + shift[1:2, :]
    proj = dot(y, win[1], 1, 0)
    probs, mixed = [], []
    for c in range(2):
        part = proj[c * 128 : c * 128 + 128]
        probs.append(probabilities(part[:, 0:128], part[:, 128:256], bias, True))
        mixed.append(mix(probs[c], part[:, 256:384], True))
    mixed = jnp.concatenate(mixed)
    sig = jax.nn.sigmoid(proj[:, 384:512] + gate[1:2, :])
    gated = sig * mixed
    final = x + dot(gated, wout[1], 1, 0)
    dgated = dot(up, wout[1], 1, 1)
    dout = dot(gated, up, 0, 0)
    dmixed = dgated * sig
    dgate = dgated * mixed * sig * (1.0 - sig)
    dproj, dbias = [], 0.0
    for c in range(2):
        part = proj[c * 128 : c * 128 + 128]
        ds, dq, dk, dv = attention_back(
            dmixed[c * 128 : c * 128 + 128],
            part[:, 0:128],
            part[:, 128:256],
            part[:, 256:384],
            probs[c],
            True,
        )
        dbias = dbias + ds
        dproj.append(jnp.concatenate([dq, dk, dv, dgate[c * 128 : c * 128 + 128]], axis=1))
    dproj = jnp.concatenate(dproj)
    din = dot(y, dproj, 0, 0)
    dx = up + norm_back(dot(dproj, win[1], 1, 1), gain[1:2, :], unit, root)
    for c in range(2):
        scatter_rows(send, (c, 2 + c), 16, dx[c * 128 : c * 128 + 128])
        scatter_rows(send, (12 + c, 14 + c), 16, final[c * 128 : c * 128 + 128])
    for h in range(4):
        scatter_rows(send, (4 + h, 8 + h), 16, dbias[h * 128 : h * 128 + 128])
    for e in range(4):
        wgrad[e * 128 : e * 128 + 128, :] = din[:, e * 128 : e * 128 + 128]
    wgrad[512:640, :] = dout


def third_kernel(
    recv, xin, first, proj_s, probs_s, mixed_s, wgrad, small, win, wout, send, dx_o, final_o, gb1_o
):
    gain, shift, gate, wbias = vectors(small)
    for r in range(2):
        for c in range(2):
            final_o[pl.ds(r * 128 + c, 64, stride=2), :] = recv[pl.ds(12 + 2 * r + c, 64, stride=16), :]
    summed = jnp.sum(recv[...].reshape(64, 16, 128)[:, 4:12, :], axis=0)
    unit1, root1 = norm_parts(first[...])
    y1 = unit1 * gain[1:2, :] + shift[1:2, :]
    dy1 = jnp.concatenate([dot(summed[4 * r : 4 * r + 4], wbias[1], 0, 0) for r in range(2)])
    gb1 = dot(summed[0:4], y1[:128], 1, 0) + dot(summed[4:8], y1[128:], 1, 0)
    up = jnp.concatenate([gather_rows(recv, (2 * r, 2 * r + 1), 16) for r in range(2)])
    up = up + norm_back(dy1, gain[1:2, :], unit1, root1)
    unit, root = norm_parts(xin[...])
    y = unit * gain[0:1, :] + shift[0:1, :]
    proj = proj_s[...]
    mixed = mixed_s[...]
    sig = jax.nn.sigmoid(proj[:, 384:512] + gate[0:1, :])
    dgated = dot(up, wout[0], 1, 1)
    dout = dot(sig * mixed, up, 0, 0)
    dmixed = dgated * sig
    dgate = dgated * mixed * sig * (1.0 - sig)
    dproj, dbias = [], 0.0
    for r in range(2):
        part = proj[r * 128 : r * 128 + 128]
        ds, dq, dk, dv = attention_back(
            dmixed[r * 128 : r * 128 + 128],
            part[:, 0:128],
            part[:, 128:256],
            part[:, 256:384],
            probs_s[r * 512 : r * 512 + 512, :],
            False,
        )
        dbias = dbias + ds
        dproj.append(jnp.concatenate([dq, dk, dv, dgate[r * 128 : r * 128 + 128]], axis=1))
    dproj = jnp.concatenate(dproj)
    din = dot(y, dproj, 0, 0)
    dx_o[...] = up + norm_back(dot(dproj, win[0], 1, 1), gain[0:1, :], unit, root)
    for h in range(4):
        scatter_rows(send, (h, 4 + h), 28, dbias[h * 128 : h * 128 + 128])
    for i in range(10):
        source = din[64 * (i % 2) : 64 * (i % 2) + 64, 128 * (i // 2) : 128 * (i // 2) + 128] if i < 8 else dout[64 * (i - 8) : 64 * (i - 8) + 64]
        send[pl.ds(8 + i, 64, stride=28), :] = source
        send[pl.ds(18 + i, 64, stride=28), :] = wgrad[64 * i : 64 * i + 64, :]
    gb1_o[0:4, :] = gb1
    gb1_o[4:8, :] = gb1


def fourth_kernel(recv, x, gb1, small, shares, totals):
    gain, shift, _, _ = vectors(small)
    pair_sum = jnp.sum(recv[...].reshape(32, 56, 128), axis=0)
    total = pair_sum[0:28] + pair_sum[28:56]
    unit, root = norm_parts(x[...])
    y = unit * gain[0:1, :] + shift[0:1, :]
    gb0 = dot(total[0:4], y[:128], 1, 0) + dot(total[4:8], y[128:], 1, 0)
    totals[...] = total[0:8]
    share = jnp.concatenate([total[8:28], gb0, gb1[0:4, :], jnp.zeros((4, 128), f32)], axis=0) * (1.0 / 128)
    for k in range(4):
        shares[32 * k : 32 * k + 32, :] = share


def tail_kernel(shares, totals, x, dx_s, final, small, share, done):
    gain, _, _, wbias = vectors(small)
    unit, root = norm_parts(x[...])
    dy = jnp.concatenate([dot(totals[4 * r : 4 * r + 4, :], wbias[0], 0, 0) for r in range(2)])
    dx = dx_s[...] + norm_back(dy, gain[0:1, :], unit, root)
    for r in range(2):
        scatter_rows(done, (r * 128, r * 128 + 1), 2, dx[r * 128 : r * 128 + 128])
    done[256:512, :] = final[...]
    for k in range(4):
        share[20 * k : 20 * k + 20, :] = shares[32 * k : 32 * k + 20, :]
    share[80:88, :] = jnp.sum(shares[...].reshape(4, 32, 128)[:, 20:28, :], axis=0)


def spread_kernel(share, out):
    for b in range(16):
        out[88 * b : 88 * b + 88, :] = share[...]


def emit_kernel(done, grad_o, final_o, mark):
    grad_o[...] = done[0:256, :]
    final_o[...] = done[256:512, :]
    mark[...] = done[0:8, :]


def last_kernel(recv, mark, gin, gbias, gout, rows):
    for j in range(20):
        for k in range(4):
            rows[pl.ds(64 * j + k, 16, stride=4), :] = recv[pl.ds(20 * k + j, 16, stride=88), :]
    for m in range(2):
        for e in range(4):
            first = 640 * m + 128 * e
            gin[m, :, 128 * e : 128 * e + 128] = rows[first : first + 128, :]
        gout[m] = rows[640 * m + 512 : 640 * m + 640, :]
    both_bias = jnp.sum(recv[...].reshape(16, 88, 128), axis=0)[80:88]
    gbias[0] = both_bias[0:4]
    gbias[1] = both_bias[4:8]


def call(kernel, outs, *args, cost=None, scratch=()):
    return pl.pallas_call(
        kernel,
        out_shape=tuple(jax.ShapeDtypeStruct(s, f32) for s in outs),
        in_specs=[pl.BlockSpec(memory_space=pltpu.VMEM)] * len(args),
        out_specs=tuple(pl.BlockSpec(memory_space=pltpu.VMEM) for _ in outs),
        scratch_shapes=scratch,
        cost_estimate=cost,
        compiler_params=pltpu.CompilerParams(vmem_limit_bytes=48 * 1024 * 1024),
    )(*args)


def solution(mesh):
    placed, there, back, fours, planes = plans(mesh)

    def swap(a, groups):
        each = a.shape[0] // len(groups[0])
        tile = 8 if each % 8 == 0 else 4
        cut = a.reshape(a.shape[0] // tile, tile, 128) if tile == 4 else a.reshape(-1, each, 128)
        got = lax.all_to_all(cut, both, 0, 0, axis_index_groups=groups, tiled=True)
        return got.reshape(a.shape)

    def body(pair, cotangent, gain, shift, win, wb, gate, wout):
        wbias = jnp.transpose(wb, (0, 2, 1)).reshape(8, 128)
        small = jnp.concatenate([gain, shift, gate, jnp.zeros_like(gate), wbias])
        xin = lax.ppermute(pair.reshape(256, 128), both, there)
        cot = lax.ppermute(cotangent.reshape(256, 128), both, there)
        (bsend,) = call(start_kernel, [(512, 128)], xin, small)
        brecv = swap(bsend, placed)
        x, proj, logits = call(
            project_kernel,
            [(256, 128), (256, 512), (1024, 128)],
            *(xin, cot, small, win),
            cost=LONG,
        )
        send1, probs, mixed, first = call(
            first_kernel,
            [(1024, 128), (1024, 128), (256, 128), (256, 128)],
            *(x, cot, brecv, proj, logits, small, wout),
        )
        recv1 = swap(send1, placed)
        send2, wgrad = call(
            second_kernel, [(1024, 128), (640, 128)], recv1, small, win, wout
        )
        recv2 = swap(send2, placed)
        send3, dx, final, gb1 = call(
            third_kernel,
            [(1792, 128), (256, 128), (256, 128), (8, 128)],
            *(recv2, x, first, proj, probs, mixed, wgrad, small, win, wout),
        )
        recv3 = swap(send3, placed)
        shares, totals = call(
            fourth_kernel, [(128, 128), (8, 128)], recv3, x, gb1, small
        )
        share, done = call(
            tail_kernel,
            [(88, 128), (512, 128)],
            *(swap(shares, fours), totals, x, dx, final, small),
        )
        share = lax.ppermute(share, both, back)
        done = lax.ppermute(done, both, back)
        (spread,) = call(spread_kernel, [(1408, 128)], share, cost=LONG)
        recv4 = swap(spread, planes)
        grad, final, mark = call(
            emit_kernel, [(256, 128), (256, 128), (8, 128)], done, cost=LONG
        )
        gin, gbias, gout = call(
            last_kernel,
            [(2, 128, 512), (2, 4, 128), (2, 128, 128)],
            *(recv4, mark),
            scratch=[pltpu.VMEM((1280, 128), f32)],
        )
        return (
            final.reshape(2, 128, 128),
            grad.reshape(2, 128, 128),
            gin,
            jnp.transpose(gbias, (0, 2, 1)),
            gout,
        )

    rows = P(("dp", "axial"), None, None)
    part = P("dp", None, None)
    return jax.shard_map(
        body,
        mesh=mesh,
        in_specs=(rows, rows, P(), P(), P(), P(), P(), P()),
        out_specs=(rows, rows, part, part, part),
        check_vma=False,
    )
```

```python
import jax
import jax.numpy as jnp
from jax import lax
from jax.experimental import pallas as pl
from jax.experimental.pallas import tpu as pltpu
from jax.sharding import PartitionSpec as P

f32 = jnp.float32
both = ("dp", "axial")
homes = (
    (5, (2, 0, 1, 3)),
    (7, (2, 3, 0, 1)),
    (1, (0, 2, 3, 1)),
    (3, (0, 1, 2, 3)),
    (6, (2, 0, 1, 3)),
    (0, (2, 3, 0, 1)),
    (4, (0, 1, 2, 3)),
    (2, (0, 2, 3, 1)),
)


def compact_id(part, rank):
    block, places = homes[part]
    place = places[rank % 4]
    z = 2 * block + place // 2
    return ((z % 4) * 2 + place % 2) * 64 + (rank // 4) * 4 + z // 4


def plans(mesh):
    parts, size = mesh.shape["dp"], mesh.shape["axial"]
    if (parts, size) == (8, 64):
        placed = [[compact_id(c, r) for r in range(64)] for c in range(8)]
    else:
        placed = [[c * size + r for r in range(size)] for c in range(parts)]
    there = [(c * size + r, placed[c][r]) for c in range(parts) for r in range(size)]
    back = [(b, a) for a, b in there]
    fours = [ids[4 * b : 4 * b + 4] for ids in placed for b in range(16)]
    planes = [[c * size + 4 * b + k for b in range(16)] for c in range(parts) for k in range(4)]
    return placed, there, back, fours, planes


def halves(a):
    if isinstance(a, tuple):
        return a
    high = a.astype(jnp.bfloat16)
    return high, (a - high.astype(f32)).astype(jnp.bfloat16)


def product(a, b, ca, cb):
    return lax.dot_general(a, b, (((ca,), (cb,)), ((), ())), preferred_element_type=f32)


def dot(a, b, ca, cb):
    (ah, al), (bh, bl) = halves(a), halves(b)
    n = bh.shape[1 - cb]
    if ca == 0:
        if n > 128:
            return product(ah, bh, 0, 0) + (product(ah, bl, 0, 0) + product(al, bh, 0, 0))
        r = product(ah, jnp.concatenate([bh, bl], axis=1), 0, 0)
        return r[:, :n] + (r[:, n:] + product(al, bh, 0, 0))
    deep = jnp.concatenate([ah, al], axis=1)
    if n != 128 or ah.shape[1] != 128:
        return product(deep, jnp.concatenate([bh, bh], axis=cb), 1, cb) + product(ah, bl, 1, cb)
    highs = jnp.concatenate([bh, bh], axis=cb)
    lows = jnp.concatenate([bl, jnp.zeros_like(bl)], axis=cb)
    r = product(deep, jnp.concatenate([highs, lows], axis=1 - cb), 1, cb)
    return r[:, :n] + r[:, n:]


def norm_parts(x):
    centre = x - jnp.mean(x, axis=-1, keepdims=True)
    root = lax.rsqrt(jnp.mean(centre * centre, axis=-1, keepdims=True) + 1e-05)
    return centre * root, root


def norm_back(dy, gain, unit, root):
    du = dy * gain
    return root * (
        du
        - jnp.mean(du, axis=-1, keepdims=True)
        - unit * jnp.mean(du * unit, axis=-1, keepdims=True)
    )


def by_head(a):
    if isinstance(a, tuple):
        return tuple(by_head(part) for part in a)
    lane = lax.broadcasted_iota(jnp.int32, (1, 128), 1) // 32
    return jnp.concatenate([a * (lane == h).astype(a.dtype) for h in range(4)], axis=0)


def side_by_side(a):
    if isinstance(a, tuple):
        return tuple(side_by_side(part) for part in a)
    return jnp.concatenate([a[128 * h : 128 * h + 128] for h in range(4)], axis=1)


SCALE = 32**-0.5
LONG = pl.CostEstimate(flops=10**11, bytes_accessed=4 * 10**8, transcendentals=0)


def probabilities(q, k, bias, keys_down):
    if keys_down:
        e = jnp.exp(dot(by_head(halves(k)), q, 1, 1) * SCALE + bias).reshape(4, 128, 128)
        return (e * (1.0 / jnp.sum(e, axis=1, keepdims=True))).reshape(512, 128)
    e = jnp.exp(dot(by_head(halves(q)), k, 1, 1) * SCALE + bias)
    return e * (1.0 / jnp.sum(e, axis=1, keepdims=True))


def mix(probs, v, keys_down):
    if keys_down:
        return dot(probs, by_head(halves(v)), 0, 0)
    return dot(side_by_side(halves(probs)), by_head(halves(v)), 1, 0)


def attention_back(do, q, k, v, probs, keys_down):
    do, q, k, v = halves(do), halves(q), halves(k), halves(v)
    split_probs = halves(probs)
    if keys_down:
        dp = dot(by_head(v), do, 1, 1)
        both_p = (probs * dp).reshape(4, 128, 128)
        ds = (both_p - probs.reshape(4, 128, 128) * jnp.sum(both_p, axis=1, keepdims=True)).reshape(
            512, 128
        )
        dv = dot(side_by_side(split_probs), by_head(do), 1, 0)
        split_ds = halves(ds)
        dk = dot(side_by_side(split_ds), by_head(q), 1, 0) * SCALE
        dq = dot(split_ds, by_head(k), 0, 0) * SCALE
    else:
        dp = dot(by_head(do), v, 1, 1)
        both_p = probs * dp
        ds = both_p - probs * jnp.sum(both_p, axis=1, keepdims=True)
        dv = dot(split_probs, by_head(do), 0, 0)
        split_ds = halves(ds)
        dk = dot(split_ds, by_head(q), 0, 0) * SCALE
        dq = dot(side_by_side(split_ds), by_head(k), 1, 0) * SCALE
    return ds, dq, dk, dv


def gather_rows(ref, first, stride):
    a, b = first
    return jnp.concatenate([ref[pl.ds(a, 64, stride=stride), :], ref[pl.ds(b, 64, stride=stride), :]])


def scatter_rows(ref, first, stride, value):
    a, b = first
    ref[pl.ds(a, 64, stride=stride), :] = value[:64]
    ref[pl.ds(b, 64, stride=stride), :] = value[64:]


def vectors(small):
    return small[0:2, :], small[2:4, :], small[4:6, :], (small[8:12, :], small[12:16, :])


def start_kernel(
    pair, cot, gain, shift, gate, wb, bias, small, packed, both_v, gain_v, shift_v, gate_v, wb_v, sems
):
    copies = [
        pltpu.make_async_copy(pair, both_v.at[pl.ds(0, 256)], sems.at[0]),
        pltpu.make_async_copy(gain, gain_v, sems.at[1]),
        pltpu.make_async_copy(shift, shift_v, sems.at[2]),
        pltpu.make_async_copy(gate, gate_v, sems.at[3]),
        pltpu.make_async_copy(wb, wb_v, sems.at[4]),
        pltpu.make_async_copy(cot, both_v.at[pl.ds(256, 256)], sems.at[5]),
    ]
    for copy in copies:
        copy.start()
    for copy in copies:
        copy.wait()
    packing = pltpu.make_async_copy(both_v, packed, sems.at[6])
    packing.start()
    gains, shifts = gain_v[...], shift_v[...]
    rows = []
    for r in range(2):
        x = gather_rows(both_v, (r * 128, r * 128 + 1), 2)
        unit, root = norm_parts(x)
        rows.append(dot(wb_v[0], unit * gains[0:1, :] + shifts[0:1, :], 1, 1))
    bias[...] = jnp.concatenate(rows, axis=0)
    small[0:8, :] = jnp.concatenate([gains, shifts, gate_v[...], jnp.zeros_like(gains)], axis=0)
    small[8:16, :] = jnp.concatenate([wb_v[0], wb_v[1]], axis=0)
    packing.wait()


def repeat_kernel(bias, out):
    block = bias[...]
    for q in range(64):
        out[q * 8 : q * 8 + 8, :] = block


def project_kernel(xin, small, win, x_o, proj_o, logits_o):
    gain, shift, _, _ = vectors(small)
    x = jnp.concatenate([gather_rows(xin, (r * 128, r * 128 + 1), 2) for r in range(2)])
    x_o[...] = x
    unit, root = norm_parts(x)
    proj = dot(unit * gain[0:1, :] + shift[0:1, :], win[0], 1, 0)
    proj_o[...] = proj
    for r in range(2):
        part = proj[r * 128 : r * 128 + 128]
        logits_o[r * 512 : r * 512 + 512, :] = (
            dot(by_head(halves(part[:, 0:128])), part[:, 128:256], 1, 1) * SCALE
        )


def first_kernel(x, xin, brecv, proj, logits, small, wout, send, probs_o, mixed_o, first_o):
    gain, shift, gate, wbias = vectors(small)
    bias = jnp.concatenate([gather_rows(brecv, (h, 4 + h), 8) for h in range(4)])
    mixed = []
    for r in range(2):
        e = jnp.exp(logits[r * 512 : r * 512 + 512, :] + bias)
        probs = e * (1.0 / jnp.sum(e, axis=1, keepdims=True))
        probs_o[r * 512 : r * 512 + 512, :] = probs
        mixed.append(mix(probs, proj[r * 128 : r * 128 + 128, 256:384], False))
    mixed = jnp.concatenate(mixed)
    mixed_o[...] = mixed
    gated = jax.nn.sigmoid(proj[:, 384:512] + gate[0:1, :]) * mixed
    first = x[...] + dot(gated, wout[0], 1, 0)
    first_o[...] = first
    unit1, root1 = norm_parts(first)
    y1 = unit1 * gain[1:2, :] + shift[1:2, :]
    bias_rows = jnp.concatenate(
        [dot(wbias[1], y1[r * 128 : r * 128 + 128], 1, 1) for r in range(2)], axis=0
    )
    for q in range(64):
        send[q * 16 + 4 : q * 16 + 12, :] = bias_rows
    for r in range(2):
        scatter_rows(send, (r * 2, r * 2 + 1), 16, first[r * 128 : r * 128 + 128])
        rows = gather_rows(xin, (256 + r * 128, 256 + r * 128 + 1), 2)
        scatter_rows(send, (12 + r * 2, 12 + r * 2 + 1), 16, rows)


def second_kernel(recv, small, win, wout, send, wgrad):
    gain, shift, gate, _ = vectors(small)
    bias = jnp.concatenate([gather_rows(recv, (4 + h, 8 + h), 16) for h in range(4)])
    x = jnp.concatenate([gather_rows(recv, (c, 2 + c), 16) for c in range(2)])
    up = jnp.concatenate([gather_rows(recv, (12 + c, 14 + c), 16) for c in range(2)])
    unit, root = norm_parts(x)
    y = unit * gain[1:2, :] + shift[1:2, :]
    proj = dot(y, win[1], 1, 0)
    probs, mixed = [], []
    for c in range(2):
        part = proj[c * 128 : c * 128 + 128]
        probs.append(probabilities(part[:, 0:128], part[:, 128:256], bias, True))
        mixed.append(mix(probs[c], part[:, 256:384], True))
    mixed = jnp.concatenate(mixed)
    sig = jax.nn.sigmoid(proj[:, 384:512] + gate[1:2, :])
    gated = sig * mixed
    final = x + dot(gated, wout[1], 1, 0)
    dgated = dot(up, wout[1], 1, 1)
    dout = dot(gated, up, 0, 0)
    dmixed = dgated * sig
    dgate = dgated * mixed * sig * (1.0 - sig)
    dproj, dbias = [], 0.0
    for c in range(2):
        part = proj[c * 128 : c * 128 + 128]
        ds, dq, dk, dv = attention_back(
            dmixed[c * 128 : c * 128 + 128],
            part[:, 0:128],
            part[:, 128:256],
            part[:, 256:384],
            probs[c],
            True,
        )
        dbias = dbias + ds
        dproj.append(jnp.concatenate([dq, dk, dv, dgate[c * 128 : c * 128 + 128]], axis=1))
    dproj = jnp.concatenate(dproj)
    din = dot(y, dproj, 0, 0)
    dx = up + norm_back(dot(dproj, win[1], 1, 1), gain[1:2, :], unit, root)
    for c in range(2):
        scatter_rows(send, (c, 2 + c), 16, dx[c * 128 : c * 128 + 128])
        scatter_rows(send, (12 + c, 14 + c), 16, final[c * 128 : c * 128 + 128])
    for h in range(4):
        scatter_rows(send, (4 + h, 8 + h), 16, dbias[h * 128 : h * 128 + 128])
    for e in range(4):
        wgrad[e * 128 : e * 128 + 128, :] = din[:, e * 128 : e * 128 + 128]
    wgrad[512:640, :] = dout


def third_kernel(
    recv, xin, first, proj_s, probs_s, mixed_s, wgrad, small, win, wout, send, dx_o, final_o, gb1_o
):
    gain, shift, gate, wbias = vectors(small)
    for r in range(2):
        for c in range(2):
            final_o[pl.ds(r * 128 + c, 64, stride=2), :] = recv[pl.ds(12 + 2 * r + c, 64, stride=16), :]
    summed = jnp.sum(recv[...].reshape(64, 16, 128)[:, 4:12, :], axis=0)
    unit1, root1 = norm_parts(first[...])
    y1 = unit1 * gain[1:2, :] + shift[1:2, :]
    dy1 = jnp.concatenate([dot(summed[4 * r : 4 * r + 4], wbias[1], 0, 0) for r in range(2)])
    gb1 = dot(summed[0:4], y1[:128], 1, 0) + dot(summed[4:8], y1[128:], 1, 0)
    up = jnp.concatenate([gather_rows(recv, (2 * r, 2 * r + 1), 16) for r in range(2)])
    up = up + norm_back(dy1, gain[1:2, :], unit1, root1)
    unit, root = norm_parts(xin[...])
    y = unit * gain[0:1, :] + shift[0:1, :]
    proj = proj_s[...]
    mixed = mixed_s[...]
    sig = jax.nn.sigmoid(proj[:, 384:512] + gate[0:1, :])
    dgated = dot(up, wout[0], 1, 1)
    dout = dot(sig * mixed, up, 0, 0)
    dmixed = dgated * sig
    dgate = dgated * mixed * sig * (1.0 - sig)
    dproj, dbias = [], 0.0
    for r in range(2):
        part = proj[r * 128 : r * 128 + 128]
        ds, dq, dk, dv = attention_back(
            dmixed[r * 128 : r * 128 + 128],
            part[:, 0:128],
            part[:, 128:256],
            part[:, 256:384],
            probs_s[r * 512 : r * 512 + 512, :],
            False,
        )
        dbias = dbias + ds
        dproj.append(jnp.concatenate([dq, dk, dv, dgate[r * 128 : r * 128 + 128]], axis=1))
    dproj = jnp.concatenate(dproj)
    din = dot(y, dproj, 0, 0)
    dx_o[...] = up + norm_back(dot(dproj, win[0], 1, 1), gain[0:1, :], unit, root)
    for h in range(4):
        scatter_rows(send, (h, 4 + h), 28, dbias[h * 128 : h * 128 + 128])
    for i in range(10):
        source = din[64 * (i % 2) : 64 * (i % 2) + 64, 128 * (i // 2) : 128 * (i // 2) + 128] if i < 8 else dout[64 * (i - 8) : 64 * (i - 8) + 64]
        send[pl.ds(8 + i, 64, stride=28), :] = source
        send[pl.ds(18 + i, 64, stride=28), :] = wgrad[64 * i : 64 * i + 64, :]
    gb1_o[0:4, :] = gb1
    gb1_o[4:8, :] = gb1


def fourth_kernel(recv, x, gb1, small, shares, totals):
    gain, shift, _, _ = vectors(small)
    pair_sum = jnp.sum(recv[...].reshape(32, 56, 128), axis=0)
    total = pair_sum[0:28] + pair_sum[28:56]
    unit, root = norm_parts(x[...])
    y = unit * gain[0:1, :] + shift[0:1, :]
    gb0 = dot(total[0:4], y[:128], 1, 0) + dot(total[4:8], y[128:], 1, 0)
    totals[...] = total[0:8]
    share = jnp.concatenate([total[8:28], gb0, gb1[0:4, :], jnp.zeros((4, 128), f32)], axis=0) * (1.0 / 128)
    for k in range(4):
        shares[32 * k : 32 * k + 32, :] = share


def tail_kernel(shares, totals, x, dx_s, final, small, share, done):
    gain, _, _, wbias = vectors(small)
    unit, root = norm_parts(x[...])
    dy = jnp.concatenate([dot(totals[4 * r : 4 * r + 4, :], wbias[0], 0, 0) for r in range(2)])
    dx = dx_s[...] + norm_back(dy, gain[0:1, :], unit, root)
    for r in range(2):
        scatter_rows(done, (r * 128, r * 128 + 1), 2, dx[r * 128 : r * 128 + 128])
    done[256:512, :] = final[...]
    for k in range(4):
        share[20 * k : 20 * k + 20, :] = shares[32 * k : 32 * k + 20, :]
    share[80:88, :] = jnp.sum(shares[...].reshape(4, 32, 128)[:, 20:28, :], axis=0)


def spread_kernel(share, out):
    for b in range(16):
        out[88 * b : 88 * b + 88, :] = share[...]


def emit_kernel(done, grad_o, final_o, mark):
    grad_o[...] = done[0:256, :]
    final_o[...] = done[256:512, :]
    mark[...] = done[0:8, :]


def last_kernel(recv, mark, gin, gbias, gout, rows):
    for j in range(20):
        for k in range(4):
            rows[pl.ds(64 * j + k, 16, stride=4), :] = recv[pl.ds(20 * k + j, 16, stride=88), :]
    for m in range(2):
        for e in range(4):
            first = 640 * m + 128 * e
            gin[m, :, 128 * e : 128 * e + 128] = rows[first : first + 128, :]
        gout[m] = rows[640 * m + 512 : 640 * m + 640, :]
    both_bias = jnp.sum(recv[...].reshape(16, 88, 128), axis=0)[80:88]
    gbias[0] = both_bias[0:4]
    gbias[1] = both_bias[4:8]


def call(kernel, outs, *args, cost=None, scratch=()):
    return pl.pallas_call(
        kernel,
        out_shape=tuple(jax.ShapeDtypeStruct(s, f32) for s in outs),
        in_specs=[pl.BlockSpec(memory_space=pltpu.VMEM)] * len(args),
        out_specs=tuple(pl.BlockSpec(memory_space=pltpu.VMEM) for _ in outs),
        scratch_shapes=scratch,
        cost_estimate=cost,
        compiler_params=pltpu.CompilerParams(vmem_limit_bytes=48 * 1024 * 1024),
    )(*args)


def solution(mesh):
    placed, there, back, fours, planes = plans(mesh)

    def swap(a, groups):
        each = a.shape[0] // len(groups[0])
        tile = 8 if each % 8 == 0 else 4
        cut = a.reshape(a.shape[0] // tile, tile, 128) if tile == 4 else a.reshape(-1, each, 128)
        got = lax.all_to_all(cut, both, 0, 0, axis_index_groups=groups, tiled=True)
        return got.reshape(a.shape)

    def body(pair, cotangent, gain, shift, win, wb, gate, wout):
        pair, cotangent = pair.reshape(256, 128), cotangent.reshape(256, 128)
        wbias = jnp.transpose(wb, (0, 2, 1))
        bias, small, packed = pl.pallas_call(
            start_kernel,
            out_shape=(
                jax.ShapeDtypeStruct((8, 128), f32),
                jax.ShapeDtypeStruct((16, 128), f32),
                jax.ShapeDtypeStruct((512, 128), f32),
            ),
            in_specs=[pl.BlockSpec(memory_space=pl.ANY)] * 6,
            out_specs=(
                pl.BlockSpec(memory_space=pltpu.VMEM),
                pl.BlockSpec(memory_space=pltpu.VMEM),
                pl.BlockSpec(memory_space=pl.ANY),
            ),
            scratch_shapes=[
                pltpu.VMEM((512, 128), f32),
                pltpu.VMEM((2, 128), f32),
                pltpu.VMEM((2, 128), f32),
                pltpu.VMEM((2, 128), f32),
                pltpu.VMEM((2, 4, 128), f32),
                pltpu.SemaphoreType.DMA((7,)),
            ],
            compiler_params=pltpu.CompilerParams(vmem_limit_bytes=60 * 1024 * 1024),
        )(pair, cotangent, gain, shift, gate, wbias)
        bias = lax.ppermute(bias, both, there)
        xin = lax.ppermute(packed, both, there)
        (repeated,) = call(repeat_kernel, [(512, 128)], bias, cost=LONG)
        brecv = swap(repeated, placed)
        x, proj, logits = call(
            project_kernel,
            [(256, 128), (256, 512), (1024, 128)],
            *(xin, small, win),
            cost=LONG,
        )
        send1, probs, mixed, first = call(
            first_kernel,
            [(1024, 128), (1024, 128), (256, 128), (256, 128)],
            *(x, xin, brecv, proj, logits, small, wout),
        )
        recv1 = swap(send1, placed)
        send2, wgrad = call(
            second_kernel, [(1024, 128), (640, 128)], recv1, small, win, wout
        )
        recv2 = swap(send2, placed)
        send3, dx, final, gb1 = call(
            third_kernel,
            [(1792, 128), (256, 128), (256, 128), (8, 128)],
            *(recv2, x, first, proj, probs, mixed, wgrad, small, win, wout),
        )
        recv3 = swap(send3, placed)
        shares, totals = call(
            fourth_kernel, [(128, 128), (8, 128)], recv3, x, gb1, small
        )
        share, done = call(
            tail_kernel,
            [(88, 128), (512, 128)],
            *(swap(shares, fours), totals, x, dx, final, small),
        )
        share = lax.ppermute(share, both, back)
        done = lax.ppermute(done, both, back)
        (spread,) = call(spread_kernel, [(1408, 128)], share, cost=LONG)
        recv4 = swap(spread, planes)
        grad, final, mark = call(
            emit_kernel, [(256, 128), (256, 128), (8, 128)], done, cost=LONG
        )
        gin, gbias, gout = call(
            last_kernel,
            [(2, 128, 512), (2, 4, 128), (2, 128, 128)],
            *(recv4, mark),
            scratch=[pltpu.VMEM((1280, 128), f32)],
        )
        return (
            final.reshape(2, 128, 128),
            grad.reshape(2, 128, 128),
            gin,
            jnp.transpose(gbias, (0, 2, 1)),
            gout,
        )

    rows = P(("dp", "axial"), None, None)
    part = P("dp", None, None)
    return jax.shard_map(
        body,
        mesh=mesh,
        in_specs=(rows, rows, P(), P(), P(), P(), P(), P()),
        out_specs=(rows, rows, part, part, part),
        check_vma=False,
    )
```

```python
import jax
import jax.numpy as jnp
from jax import lax
from jax.experimental import pallas as pl
from jax.experimental.pallas import tpu as pltpu
from jax.sharding import PartitionSpec as P

f32 = jnp.float32
both = ("dp", "axial")
homes = (
    (5, (2, 0, 1, 3)),
    (7, (2, 3, 0, 1)),
    (1, (0, 2, 3, 1)),
    (3, (0, 1, 2, 3)),
    (6, (2, 0, 1, 3)),
    (0, (2, 3, 0, 1)),
    (4, (0, 1, 2, 3)),
    (2, (0, 2, 3, 1)),
)


def compact_id(part, rank):
    block, places = homes[part]
    place = places[rank % 4]
    z = 2 * block + place // 2
    return ((z % 4) * 2 + place % 2) * 64 + (rank // 4) * 4 + z // 4


def plans(mesh):
    parts, size = mesh.shape["dp"], mesh.shape["axial"]
    if (parts, size) == (8, 64):
        placed = [[compact_id(c, r) for r in range(64)] for c in range(8)]
    else:
        placed = [[c * size + r for r in range(size)] for c in range(parts)]
    there = [(c * size + r, placed[c][r]) for c in range(parts) for r in range(size)]
    back = [(b, a) for a, b in there]
    fours = [ids[4 * b : 4 * b + 4] for ids in placed for b in range(16)]
    planes = [[c * size + 4 * b + k for b in range(16)] for c in range(parts) for k in range(4)]
    return placed, there, back, fours, planes


def halves(a):
    if isinstance(a, tuple):
        return a
    high = a.astype(jnp.bfloat16)
    return high, (a - high.astype(f32)).astype(jnp.bfloat16)


def product(a, b, ca, cb):
    return lax.dot_general(a, b, (((ca,), (cb,)), ((), ())), preferred_element_type=f32)


def dot(a, b, ca, cb):
    (ah, al), (bh, bl) = halves(a), halves(b)
    n = bh.shape[1 - cb]
    if ca == 0:
        if n > 128:
            return product(ah, bh, 0, 0) + (product(ah, bl, 0, 0) + product(al, bh, 0, 0))
        r = product(ah, jnp.concatenate([bh, bl], axis=1), 0, 0)
        return r[:, :n] + (r[:, n:] + product(al, bh, 0, 0))
    deep = jnp.concatenate([ah, al], axis=1)
    if n != 128 or ah.shape[1] != 128:
        return product(deep, jnp.concatenate([bh, bh], axis=cb), 1, cb) + product(ah, bl, 1, cb)
    highs = jnp.concatenate([bh, bh], axis=cb)
    lows = jnp.concatenate([bl, jnp.zeros_like(bl)], axis=cb)
    r = product(deep, jnp.concatenate([highs, lows], axis=1 - cb), 1, cb)
    return r[:, :n] + r[:, n:]


def norm_parts(x):
    centre = x - jnp.mean(x, axis=-1, keepdims=True)
    root = lax.rsqrt(jnp.mean(centre * centre, axis=-1, keepdims=True) + 1e-05)
    return centre * root, root


def norm_back(dy, gain, unit, root):
    du = dy * gain
    return root * (
        du
        - jnp.mean(du, axis=-1, keepdims=True)
        - unit * jnp.mean(du * unit, axis=-1, keepdims=True)
    )


def by_head(a):
    if isinstance(a, tuple):
        return tuple(by_head(part) for part in a)
    lane = lax.broadcasted_iota(jnp.int32, (1, 128), 1) // 32
    return jnp.concatenate([a * (lane == h).astype(a.dtype) for h in range(4)], axis=0)


def side_by_side(a):
    if isinstance(a, tuple):
        return tuple(side_by_side(part) for part in a)
    return jnp.concatenate([a[128 * h : 128 * h + 128] for h in range(4)], axis=1)


SCALE = 32**-0.5
LONG = pl.CostEstimate(flops=10**11, bytes_accessed=4 * 10**8, transcendentals=0)


def probabilities(q, k, bias, keys_down):
    if keys_down:
        e = jnp.exp(dot(by_head(halves(k)), q, 1, 1) * SCALE + bias).reshape(4, 128, 128)
        return (e * (1.0 / jnp.sum(e, axis=1, keepdims=True))).reshape(512, 128)
    e = jnp.exp(dot(by_head(halves(q)), k, 1, 1) * SCALE + bias)
    return e * (1.0 / jnp.sum(e, axis=1, keepdims=True))


def mix(probs, v, keys_down):
    if keys_down:
        return dot(probs, by_head(halves(v)), 0, 0)
    return dot(side_by_side(halves(probs)), by_head(halves(v)), 1, 0)


def attention_back(do, q, k, v, probs, keys_down):
    do, q, k, v = halves(do), halves(q), halves(k), halves(v)
    split_probs = halves(probs)
    if keys_down:
        dp = dot(by_head(v), do, 1, 1)
        both_p = (probs * dp).reshape(4, 128, 128)
        ds = (both_p - probs.reshape(4, 128, 128) * jnp.sum(both_p, axis=1, keepdims=True)).reshape(
            512, 128
        )
        dv = dot(side_by_side(split_probs), by_head(do), 1, 0)
        split_ds = halves(ds)
        dk = dot(side_by_side(split_ds), by_head(q), 1, 0) * SCALE
        dq = dot(split_ds, by_head(k), 0, 0) * SCALE
    else:
        dp = dot(by_head(do), v, 1, 1)
        both_p = probs * dp
        ds = both_p - probs * jnp.sum(both_p, axis=1, keepdims=True)
        dv = dot(split_probs, by_head(do), 0, 0)
        split_ds = halves(ds)
        dk = dot(split_ds, by_head(q), 0, 0) * SCALE
        dq = dot(side_by_side(split_ds), by_head(k), 1, 0) * SCALE
    return ds, dq, dk, dv


def gather_rows(ref, first, stride):
    a, b = first
    return jnp.concatenate([ref[pl.ds(a, 64, stride=stride), :], ref[pl.ds(b, 64, stride=stride), :]])


def scatter_rows(ref, first, stride, value):
    a, b = first
    ref[pl.ds(a, 64, stride=stride), :] = value[:64]
    ref[pl.ds(b, 64, stride=stride), :] = value[64:]


def vectors(small):
    return small[0:2, :], small[2:4, :], small[4:6, :], (small[8:12, :], small[12:16, :])


def start_kernel(
    pair, cot, gain, shift, gate, wb, bias, small, packed, both_v, gain_v, shift_v, gate_v, wb_v, sems
):
    copies = [
        pltpu.make_async_copy(pair, both_v.at[pl.ds(0, 256)], sems.at[0]),
        pltpu.make_async_copy(gain, gain_v, sems.at[1]),
        pltpu.make_async_copy(shift, shift_v, sems.at[2]),
        pltpu.make_async_copy(gate, gate_v, sems.at[3]),
        pltpu.make_async_copy(wb, wb_v, sems.at[4]),
        pltpu.make_async_copy(cot, both_v.at[pl.ds(256, 256)], sems.at[5]),
    ]
    for copy in copies:
        copy.start()
    for copy in copies[:5]:
        copy.wait()
    packing = [
        pltpu.make_async_copy(
            both_v.at[pl.ds(256 * i, 256)], packed.at[pl.ds(256 * i, 256)], sems.at[6 + i]
        )
        for i in range(2)
    ]
    packing[0].start()
    copies[5].wait()
    packing[1].start()
    gains, shifts = gain_v[...], shift_v[...]
    rows = []
    for r in range(2):
        x = gather_rows(both_v, (r * 128, r * 128 + 1), 2)
        unit, root = norm_parts(x)
        rows.append(dot(wb_v[0], unit * gains[0:1, :] + shifts[0:1, :], 1, 1))
    bias[...] = jnp.concatenate(rows, axis=0)
    small[0:8, :] = jnp.concatenate([gains, shifts, gate_v[...], jnp.zeros_like(gains)], axis=0)
    small[8:16, :] = jnp.concatenate([wb_v[0], wb_v[1]], axis=0)
    for copy in packing:
        copy.wait()


def repeat_kernel(bias, out):
    block = bias[...]
    for q in range(64):
        out[q * 8 : q * 8 + 8, :] = block


def project_kernel(xin, small, win, x_o, proj_o, logits_o):
    gain, shift, _, _ = vectors(small)
    x = jnp.concatenate([gather_rows(xin, (r * 128, r * 128 + 1), 2) for r in range(2)])
    x_o[...] = x
    unit, root = norm_parts(x)
    proj = dot(unit * gain[0:1, :] + shift[0:1, :], win[0], 1, 0)
    proj_o[...] = proj
    for r in range(2):
        part = proj[r * 128 : r * 128 + 128]
        logits_o[r * 512 : r * 512 + 512, :] = (
            dot(by_head(halves(part[:, 0:128])), part[:, 128:256], 1, 1) * SCALE
        )


def first_kernel(x, xin, brecv, proj, logits, small, wout, send, probs_o, mixed_o, first_o):
    gain, shift, gate, wbias = vectors(small)
    bias = jnp.concatenate([gather_rows(brecv, (h, 4 + h), 8) for h in range(4)])
    mixed = []
    for r in range(2):
        e = jnp.exp(logits[r * 512 : r * 512 + 512, :] + bias)
        probs = e * (1.0 / jnp.sum(e, axis=1, keepdims=True))
        probs_o[r * 512 : r * 512 + 512, :] = probs
        mixed.append(mix(probs, proj[r * 128 : r * 128 + 128, 256:384], False))
    mixed = jnp.concatenate(mixed)
    mixed_o[...] = mixed
    gated = jax.nn.sigmoid(proj[:, 384:512] + gate[0:1, :]) * mixed
    first = x[...] + dot(gated, wout[0], 1, 0)
    first_o[...] = first
    unit1, root1 = norm_parts(first)
    y1 = unit1 * gain[1:2, :] + shift[1:2, :]
    bias_rows = jnp.concatenate(
        [dot(wbias[1], y1[r * 128 : r * 128 + 128], 1, 1) for r in range(2)], axis=0
    )
    for q in range(64):
        send[q * 16 + 4 : q * 16 + 12, :] = bias_rows
    for r in range(2):
        scatter_rows(send, (r * 2, r * 2 + 1), 16, first[r * 128 : r * 128 + 128])
        rows = gather_rows(xin, (256 + r * 128, 256 + r * 128 + 1), 2)
        scatter_rows(send, (12 + r * 2, 12 + r * 2 + 1), 16, rows)


def second_kernel(recv, small, win, wout, send, wgrad):
    gain, shift, gate, _ = vectors(small)
    bias = jnp.concatenate([gather_rows(recv, (4 + h, 8 + h), 16) for h in range(4)])
    x = jnp.concatenate([gather_rows(recv, (c, 2 + c), 16) for c in range(2)])
    up = jnp.concatenate([gather_rows(recv, (12 + c, 14 + c), 16) for c in range(2)])
    unit, root = norm_parts(x)
    y = unit * gain[1:2, :] + shift[1:2, :]
    proj = dot(y, win[1], 1, 0)
    probs, mixed = [], []
    for c in range(2):
        part = proj[c * 128 : c * 128 + 128]
        probs.append(probabilities(part[:, 0:128], part[:, 128:256], bias, True))
        mixed.append(mix(probs[c], part[:, 256:384], True))
    mixed = jnp.concatenate(mixed)
    sig = jax.nn.sigmoid(proj[:, 384:512] + gate[1:2, :])
    gated = sig * mixed
    final = x + dot(gated, wout[1], 1, 0)
    dgated = dot(up, wout[1], 1, 1)
    dout = dot(gated, up, 0, 0)
    dmixed = dgated * sig
    dgate = dgated * mixed * sig * (1.0 - sig)
    dproj, dbias = [], 0.0
    for c in range(2):
        part = proj[c * 128 : c * 128 + 128]
        ds, dq, dk, dv = attention_back(
            dmixed[c * 128 : c * 128 + 128],
            part[:, 0:128],
            part[:, 128:256],
            part[:, 256:384],
            probs[c],
            True,
        )
        dbias = dbias + ds
        dproj.append(jnp.concatenate([dq, dk, dv, dgate[c * 128 : c * 128 + 128]], axis=1))
    dproj = jnp.concatenate(dproj)
    din = dot(y, dproj, 0, 0)
    dx = up + norm_back(dot(dproj, win[1], 1, 1), gain[1:2, :], unit, root)
    for c in range(2):
        scatter_rows(send, (c, 2 + c), 16, dx[c * 128 : c * 128 + 128])
        scatter_rows(send, (12 + c, 14 + c), 16, final[c * 128 : c * 128 + 128])
    for h in range(4):
        scatter_rows(send, (4 + h, 8 + h), 16, dbias[h * 128 : h * 128 + 128])
    for e in range(4):
        wgrad[e * 128 : e * 128 + 128, :] = din[:, e * 128 : e * 128 + 128]
    wgrad[512:640, :] = dout


def third_kernel(
    recv, xin, first, proj_s, probs_s, mixed_s, wgrad, small, win, wout, send, dx_o, final_o, gb1_o
):
    gain, shift, gate, wbias = vectors(small)
    for r in range(2):
        for c in range(2):
            final_o[pl.ds(r * 128 + c, 64, stride=2), :] = recv[pl.ds(12 + 2 * r + c, 64, stride=16), :]
    summed = jnp.sum(recv[...].reshape(64, 16, 128)[:, 4:12, :], axis=0)
    unit1, root1 = norm_parts(first[...])
    y1 = unit1 * gain[1:2, :] + shift[1:2, :]
    dy1 = jnp.concatenate([dot(summed[4 * r : 4 * r + 4], wbias[1], 0, 0) for r in range(2)])
    gb1 = dot(summed[0:4], y1[:128], 1, 0) + dot(summed[4:8], y1[128:], 1, 0)
    up = jnp.concatenate([gather_rows(recv, (2 * r, 2 * r + 1), 16) for r in range(2)])
    up = up + norm_back(dy1, gain[1:2, :], unit1, root1)
    unit, root = norm_parts(xin[...])
    y = unit * gain[0:1, :] + shift[0:1, :]
    proj = proj_s[...]
    mixed = mixed_s[...]
    sig = jax.nn.sigmoid(proj[:, 384:512] + gate[0:1, :])
    dgated = dot(up, wout[0], 1, 1)
    dout = dot(sig * mixed, up, 0, 0)
    dmixed = dgated * sig
    dgate = dgated * mixed * sig * (1.0 - sig)
    dproj, dbias = [], 0.0
    for r in range(2):
        part = proj[r * 128 : r * 128 + 128]
        ds, dq, dk, dv = attention_back(
            dmixed[r * 128 : r * 128 + 128],
            part[:, 0:128],
            part[:, 128:256],
            part[:, 256:384],
            probs_s[r * 512 : r * 512 + 512, :],
            False,
        )
        dbias = dbias + ds
        dproj.append(jnp.concatenate([dq, dk, dv, dgate[r * 128 : r * 128 + 128]], axis=1))
    dproj = jnp.concatenate(dproj)
    din = dot(y, dproj, 0, 0)
    dx_o[...] = up + norm_back(dot(dproj, win[0], 1, 1), gain[0:1, :], unit, root)
    for h in range(4):
        scatter_rows(send, (h, 4 + h), 28, dbias[h * 128 : h * 128 + 128])
    for i in range(10):
        source = din[64 * (i % 2) : 64 * (i % 2) + 64, 128 * (i // 2) : 128 * (i // 2) + 128] if i < 8 else dout[64 * (i - 8) : 64 * (i - 8) + 64]
        send[pl.ds(8 + i, 64, stride=28), :] = source
        send[pl.ds(18 + i, 64, stride=28), :] = wgrad[64 * i : 64 * i + 64, :]
    gb1_o[0:4, :] = gb1
    gb1_o[4:8, :] = gb1


def fourth_kernel(recv, x, gb1, small, shares, totals):
    gain, shift, _, _ = vectors(small)
    pair_sum = jnp.sum(recv[...].reshape(32, 56, 128), axis=0)
    total = pair_sum[0:28] + pair_sum[28:56]
    unit, root = norm_parts(x[...])
    y = unit * gain[0:1, :] + shift[0:1, :]
    gb0 = dot(total[0:4], y[:128], 1, 0) + dot(total[4:8], y[128:], 1, 0)
    totals[...] = total[0:8]
    share = jnp.concatenate([total[8:28], gb0, gb1[0:4, :], jnp.zeros((4, 128), f32)], axis=0) * (1.0 / 128)
    for k in range(4):
        shares[32 * k : 32 * k + 32, :] = share


def tail_kernel(shares, totals, x, dx_s, final, small, share, done):
    gain, _, _, wbias = vectors(small)
    unit, root = norm_parts(x[...])
    dy = jnp.concatenate([dot(totals[4 * r : 4 * r + 4, :], wbias[0], 0, 0) for r in range(2)])
    dx = dx_s[...] + norm_back(dy, gain[0:1, :], unit, root)
    for r in range(2):
        scatter_rows(done, (r * 128, r * 128 + 1), 2, dx[r * 128 : r * 128 + 128])
    done[256:512, :] = final[...]
    for k in range(4):
        share[20 * k : 20 * k + 20, :] = shares[32 * k : 32 * k + 20, :]
    share[80:88, :] = jnp.sum(shares[...].reshape(4, 32, 128)[:, 20:28, :], axis=0)


def spread_kernel(share, out):
    for b in range(16):
        out[88 * b : 88 * b + 88, :] = share[...]


def emit_kernel(done, grad_o, final_o, mark):
    grad_o[...] = done[0:256, :]
    final_o[...] = done[256:512, :]
    mark[...] = done[0:8, :]


def last_kernel(recv, mark, gin, gbias, gout, rows):
    for j in range(20):
        for k in range(4):
            rows[pl.ds(64 * j + k, 16, stride=4), :] = recv[pl.ds(20 * k + j, 16, stride=88), :]
    for m in range(2):
        for e in range(4):
            first = 640 * m + 128 * e
            gin[m, :, 128 * e : 128 * e + 128] = rows[first : first + 128, :]
        gout[m] = rows[640 * m + 512 : 640 * m + 640, :]
    both_bias = jnp.sum(recv[...].reshape(16, 88, 128), axis=0)[80:88]
    gbias[0] = both_bias[0:4]
    gbias[1] = both_bias[4:8]


def call(kernel, outs, *args, cost=None, scratch=()):
    return pl.pallas_call(
        kernel,
        out_shape=tuple(jax.ShapeDtypeStruct(s, f32) for s in outs),
        in_specs=[pl.BlockSpec(memory_space=pltpu.VMEM)] * len(args),
        out_specs=tuple(pl.BlockSpec(memory_space=pltpu.VMEM) for _ in outs),
        scratch_shapes=scratch,
        cost_estimate=cost,
        compiler_params=pltpu.CompilerParams(vmem_limit_bytes=48 * 1024 * 1024),
    )(*args)


def solution(mesh):
    placed, there, back, fours, planes = plans(mesh)

    def swap(a, groups):
        each = a.shape[0] // len(groups[0])
        tile = 8 if each % 8 == 0 else 4
        cut = a.reshape(a.shape[0] // tile, tile, 128) if tile == 4 else a.reshape(-1, each, 128)
        got = lax.all_to_all(cut, both, 0, 0, axis_index_groups=groups, tiled=True)
        return got.reshape(a.shape)

    def body(pair, cotangent, gain, shift, win, wb, gate, wout):
        pair, cotangent = pair.reshape(256, 128), cotangent.reshape(256, 128)
        wbias = jnp.transpose(wb, (0, 2, 1))
        bias, small, packed = pl.pallas_call(
            start_kernel,
            out_shape=(
                jax.ShapeDtypeStruct((8, 128), f32),
                jax.ShapeDtypeStruct((16, 128), f32),
                jax.ShapeDtypeStruct((512, 128), f32),
            ),
            in_specs=[pl.BlockSpec(memory_space=pl.ANY)] * 6,
            out_specs=(
                pl.BlockSpec(memory_space=pltpu.VMEM),
                pl.BlockSpec(memory_space=pltpu.VMEM),
                pl.BlockSpec(memory_space=pl.ANY),
            ),
            scratch_shapes=[
                pltpu.VMEM((512, 128), f32),
                pltpu.VMEM((2, 128), f32),
                pltpu.VMEM((2, 128), f32),
                pltpu.VMEM((2, 128), f32),
                pltpu.VMEM((2, 4, 128), f32),
                pltpu.SemaphoreType.DMA((8,)),
            ],
            compiler_params=pltpu.CompilerParams(vmem_limit_bytes=60 * 1024 * 1024),
        )(pair, cotangent, gain, shift, gate, wbias)
        bias = lax.ppermute(bias, both, there)
        xin = lax.ppermute(packed, both, there)
        (repeated,) = call(repeat_kernel, [(512, 128)], bias, cost=LONG)
        brecv = swap(repeated, placed)
        x, proj, logits = call(
            project_kernel,
            [(256, 128), (256, 512), (1024, 128)],
            *(xin, small, win),
            cost=LONG,
        )
        send1, probs, mixed, first = call(
            first_kernel,
            [(1024, 128), (1024, 128), (256, 128), (256, 128)],
            *(x, xin, brecv, proj, logits, small, wout),
        )
        recv1 = swap(send1, placed)
        send2, wgrad = call(
            second_kernel, [(1024, 128), (640, 128)], recv1, small, win, wout
        )
        recv2 = swap(send2, placed)
        send3, dx, final, gb1 = call(
            third_kernel,
            [(1792, 128), (256, 128), (256, 128), (8, 128)],
            *(recv2, x, first, proj, probs, mixed, wgrad, small, win, wout),
        )
        recv3 = swap(send3, placed)
        shares, totals = call(
            fourth_kernel, [(128, 128), (8, 128)], recv3, x, gb1, small
        )
        share, done = call(
            tail_kernel,
            [(88, 128), (512, 128)],
            *(swap(shares, fours), totals, x, dx, final, small),
        )
        share = lax.ppermute(share, both, back)
        done = lax.ppermute(done, both, back)
        (spread,) = call(spread_kernel, [(1408, 128)], share, cost=LONG)
        recv4 = swap(spread, planes)
        grad, final, mark = call(
            emit_kernel, [(256, 128), (256, 128), (8, 128)], done, cost=LONG
        )
        gin, gbias, gout = call(
            last_kernel,
            [(2, 128, 512), (2, 4, 128), (2, 128, 128)],
            *(recv4, mark),
            scratch=[pltpu.VMEM((1280, 128), f32)],
        )
        return (
            final.reshape(2, 128, 128),
            grad.reshape(2, 128, 128),
            gin,
            jnp.transpose(gbias, (0, 2, 1)),
            gout,
        )

    rows = P(("dp", "axial"), None, None)
    part = P("dp", None, None)
    return jax.shard_map(
        body,
        mesh=mesh,
        in_specs=(rows, rows, P(), P(), P(), P(), P(), P()),
        out_specs=(rows, rows, part, part, part),
        check_vma=False,
    )
```

```python
import jax
import jax.numpy as jnp
from jax import lax
from jax.experimental import pallas as pl
from jax.experimental.pallas import tpu as pltpu
from jax.sharding import PartitionSpec as P

f32 = jnp.float32
both = ("dp", "axial")
homes = (
    (5, (2, 0, 1, 3)),
    (7, (2, 3, 0, 1)),
    (1, (0, 2, 3, 1)),
    (3, (0, 1, 2, 3)),
    (6, (2, 0, 1, 3)),
    (0, (2, 3, 0, 1)),
    (4, (0, 1, 2, 3)),
    (2, (0, 2, 3, 1)),
)


def compact_id(part, rank):
    block, places = homes[part]
    place = places[rank % 4]
    z = 2 * block + place // 2
    return ((z % 4) * 2 + place % 2) * 64 + (rank // 4) * 4 + z // 4


def plans(mesh):
    parts, size = mesh.shape["dp"], mesh.shape["axial"]
    if (parts, size) == (8, 64):
        placed = [[compact_id(c, r) for r in range(64)] for c in range(8)]
    else:
        placed = [[c * size + r for r in range(size)] for c in range(parts)]
    there = [(c * size + r, placed[c][r]) for c in range(parts) for r in range(size)]
    back = [(b, a) for a, b in there]
    fours = [ids[4 * b : 4 * b + 4] for ids in placed for b in range(16)]
    planes = [[c * size + 4 * b + k for b in range(16)] for c in range(parts) for k in range(4)]
    return placed, there, back, fours, planes


def halves(a):
    if isinstance(a, tuple):
        return a
    high = a.astype(jnp.bfloat16)
    return high, (a - high.astype(f32)).astype(jnp.bfloat16)


def product(a, b, ca, cb):
    return lax.dot_general(a, b, (((ca,), (cb,)), ((), ())), preferred_element_type=f32)


def dot(a, b, ca, cb):
    (ah, al), (bh, bl) = halves(a), halves(b)
    n = bh.shape[1 - cb]
    if ca == 0:
        if n > 128:
            return product(ah, bh, 0, 0) + (product(ah, bl, 0, 0) + product(al, bh, 0, 0))
        r = product(ah, jnp.concatenate([bh, bl], axis=1), 0, 0)
        return r[:, :n] + (r[:, n:] + product(al, bh, 0, 0))
    deep = jnp.concatenate([ah, al], axis=1)
    if n != 128 or ah.shape[1] != 128:
        return product(deep, jnp.concatenate([bh, bh], axis=cb), 1, cb) + product(ah, bl, 1, cb)
    highs = jnp.concatenate([bh, bh], axis=cb)
    lows = jnp.concatenate([bl, jnp.zeros_like(bl)], axis=cb)
    r = product(deep, jnp.concatenate([highs, lows], axis=1 - cb), 1, cb)
    return r[:, :n] + r[:, n:]


def norm_parts(x):
    centre = x - jnp.mean(x, axis=-1, keepdims=True)
    root = lax.rsqrt(jnp.mean(centre * centre, axis=-1, keepdims=True) + 1e-05)
    return centre * root, root


def norm_back(dy, gain, unit, root):
    du = dy * gain
    return root * (
        du
        - jnp.mean(du, axis=-1, keepdims=True)
        - unit * jnp.mean(du * unit, axis=-1, keepdims=True)
    )


def by_head(a):
    if isinstance(a, tuple):
        return tuple(by_head(part) for part in a)
    lane = lax.broadcasted_iota(jnp.int32, (1, 128), 1) // 32
    return jnp.concatenate([a * (lane == h).astype(a.dtype) for h in range(4)], axis=0)


def side_by_side(a):
    if isinstance(a, tuple):
        return tuple(side_by_side(part) for part in a)
    return jnp.concatenate([a[128 * h : 128 * h + 128] for h in range(4)], axis=1)


SCALE = 32**-0.5
LONG = pl.CostEstimate(flops=10**11, bytes_accessed=4 * 10**8, transcendentals=0)


def probabilities(q, k, bias, keys_down):
    if keys_down:
        e = jnp.exp(dot(by_head(halves(k)), q, 1, 1) * SCALE + bias).reshape(4, 128, 128)
        return (e * (1.0 / jnp.sum(e, axis=1, keepdims=True))).reshape(512, 128)
    e = jnp.exp(dot(by_head(halves(q)), k, 1, 1) * SCALE + bias)
    return e * (1.0 / jnp.sum(e, axis=1, keepdims=True))


def mix(probs, v, keys_down):
    if keys_down:
        return dot(probs, by_head(halves(v)), 0, 0)
    return dot(side_by_side(halves(probs)), by_head(halves(v)), 1, 0)


def attention_back(do, q, k, v, probs, keys_down):
    do, q, k, v = halves(do), halves(q), halves(k), halves(v)
    split_probs = halves(probs)
    if keys_down:
        dp = dot(by_head(v), do, 1, 1)
        both_p = (probs * dp).reshape(4, 128, 128)
        ds = (both_p - probs.reshape(4, 128, 128) * jnp.sum(both_p, axis=1, keepdims=True)).reshape(
            512, 128
        )
        dv = dot(side_by_side(split_probs), by_head(do), 1, 0)
        split_ds = halves(ds)
        dk = dot(side_by_side(split_ds), by_head(q), 1, 0) * SCALE
        dq = dot(split_ds, by_head(k), 0, 0) * SCALE
    else:
        dp = dot(by_head(do), v, 1, 1)
        both_p = probs * dp
        ds = both_p - probs * jnp.sum(both_p, axis=1, keepdims=True)
        dv = dot(split_probs, by_head(do), 0, 0)
        split_ds = halves(ds)
        dk = dot(split_ds, by_head(q), 0, 0) * SCALE
        dq = dot(side_by_side(split_ds), by_head(k), 1, 0) * SCALE
    return ds, dq, dk, dv


def gather_rows(ref, first, stride):
    a, b = first
    return jnp.concatenate([ref[pl.ds(a, 64, stride=stride), :], ref[pl.ds(b, 64, stride=stride), :]])


def scatter_rows(ref, first, stride, value):
    a, b = first
    ref[pl.ds(a, 64, stride=stride), :] = value[:64]
    ref[pl.ds(b, 64, stride=stride), :] = value[64:]


def vectors(small):
    return small[0:2, :], small[2:4, :], small[4:6, :], (small[8:12, :], small[12:16, :])


def start_kernel(
    pair, cot, gain, shift, gate, wb, bias, small, packed, both_v, gain_v, shift_v, gate_v, wb_v, sems
):
    copies = [
        pltpu.make_async_copy(pair, both_v.at[pl.ds(0, 256)], sems.at[0]),
        pltpu.make_async_copy(gain, gain_v, sems.at[1]),
        pltpu.make_async_copy(shift, shift_v, sems.at[2]),
        pltpu.make_async_copy(gate, gate_v, sems.at[3]),
        pltpu.make_async_copy(wb, wb_v, sems.at[4]),
        pltpu.make_async_copy(cot, both_v.at[pl.ds(256, 256)], sems.at[5]),
    ]
    for copy in copies:
        copy.start()
    for copy in copies:
        copy.wait()
    packing = pltpu.make_async_copy(both_v, packed, sems.at[6])
    packing.start()
    gains, shifts = gain_v[...], shift_v[...]
    rows = []
    for r in range(2):
        x = gather_rows(both_v, (r * 128, r * 128 + 1), 2)
        unit, root = norm_parts(x)
        rows.append(dot(wb_v[0], unit * gains[0:1, :] + shifts[0:1, :], 1, 1))
    bias[...] = jnp.concatenate(rows, axis=0)
    small[0:8, :] = jnp.concatenate([gains, shifts, gate_v[...], jnp.zeros_like(gains)], axis=0)
    small[8:16, :] = jnp.concatenate([wb_v[0], wb_v[1]], axis=0)
    packing.wait()


def repeat_kernel(bias, out):
    block = bias[...]
    for q in range(64):
        out[q * 8 : q * 8 + 8, :] = block


def project_kernel(xin, small, win, x_o, proj_o, logits_o):
    gain, shift, _, _ = vectors(small)
    x = jnp.concatenate([gather_rows(xin, (r * 128, r * 128 + 1), 2) for r in range(2)])
    x_o[...] = x
    unit, root = norm_parts(x)
    proj = dot(unit * gain[0:1, :] + shift[0:1, :], win[0], 1, 0)
    proj_o[...] = proj
    for r in range(2):
        part = proj[r * 128 : r * 128 + 128]
        logits_o[r * 512 : r * 512 + 512, :] = (
            dot(by_head(halves(part[:, 0:128])), part[:, 128:256], 1, 1) * SCALE
        )


def first_kernel(x, xin, brecv, proj, logits, small, wout, send, probs_o, mixed_o, first_o):
    gain, shift, gate, wbias = vectors(small)
    bias = jnp.concatenate([gather_rows(brecv, (h, 4 + h), 8) for h in range(4)])
    mixed = []
    for r in range(2):
        e = jnp.exp(logits[r * 512 : r * 512 + 512, :] + bias)
        probs = e * (1.0 / jnp.sum(e, axis=1, keepdims=True))
        probs_o[r * 512 : r * 512 + 512, :] = probs
        mixed.append(mix(probs, proj[r * 128 : r * 128 + 128, 256:384], False))
    mixed = jnp.concatenate(mixed)
    mixed_o[...] = mixed
    gated = jax.nn.sigmoid(proj[:, 384:512] + gate[0:1, :]) * mixed
    first = x[...] + dot(gated, wout[0], 1, 0)
    first_o[...] = first
    unit1, root1 = norm_parts(first)
    y1 = unit1 * gain[1:2, :] + shift[1:2, :]
    bias_rows = jnp.concatenate(
        [dot(wbias[1], y1[r * 128 : r * 128 + 128], 1, 1) for r in range(2)], axis=0
    )
    for q in range(64):
        send[q * 16 + 4 : q * 16 + 12, :] = bias_rows
    for r in range(2):
        scatter_rows(send, (r * 2, r * 2 + 1), 16, first[r * 128 : r * 128 + 128])
        rows = gather_rows(xin, (256 + r * 128, 256 + r * 128 + 1), 2)
        scatter_rows(send, (12 + r * 2, 12 + r * 2 + 1), 16, rows)


def second_kernel(recv, small, win, wout, send, wgrad):
    gain, shift, gate, _ = vectors(small)
    bias = jnp.concatenate([gather_rows(recv, (4 + h, 8 + h), 16) for h in range(4)])
    x = jnp.concatenate([gather_rows(recv, (c, 2 + c), 16) for c in range(2)])
    up = jnp.concatenate([gather_rows(recv, (12 + c, 14 + c), 16) for c in range(2)])
    unit, root = norm_parts(x)
    y = unit * gain[1:2, :] + shift[1:2, :]
    proj = dot(y, win[1], 1, 0)
    probs, mixed = [], []
    for c in range(2):
        part = proj[c * 128 : c * 128 + 128]
        probs.append(probabilities(part[:, 0:128], part[:, 128:256], bias, True))
        mixed.append(mix(probs[c], part[:, 256:384], True))
    mixed = jnp.concatenate(mixed)
    sig = jax.nn.sigmoid(proj[:, 384:512] + gate[1:2, :])
    gated = sig * mixed
    final = x + dot(gated, wout[1], 1, 0)
    dgated = dot(up, wout[1], 1, 1)
    dout = dot(gated, up, 0, 0)
    dmixed = dgated * sig
    dgate = dgated * mixed * sig * (1.0 - sig)
    dproj, dbias = [], 0.0
    for c in range(2):
        part = proj[c * 128 : c * 128 + 128]
        ds, dq, dk, dv = attention_back(
            dmixed[c * 128 : c * 128 + 128],
            part[:, 0:128],
            part[:, 128:256],
            part[:, 256:384],
            probs[c],
            True,
        )
        dbias = dbias + ds
        dproj.append(jnp.concatenate([dq, dk, dv, dgate[c * 128 : c * 128 + 128]], axis=1))
    dproj = jnp.concatenate(dproj)
    din = dot(y, dproj, 0, 0)
    dx = up + norm_back(dot(dproj, win[1], 1, 1), gain[1:2, :], unit, root)
    for c in range(2):
        scatter_rows(send, (c, 2 + c), 16, dx[c * 128 : c * 128 + 128])
        scatter_rows(send, (12 + c, 14 + c), 16, final[c * 128 : c * 128 + 128])
    for h in range(4):
        scatter_rows(send, (4 + h, 8 + h), 16, dbias[h * 128 : h * 128 + 128])
    for e in range(4):
        wgrad[e * 128 : e * 128 + 128, :] = din[:, e * 128 : e * 128 + 128]
    wgrad[512:640, :] = dout


def third_kernel(
    recv, xin, first, proj_s, probs_s, mixed_s, wgrad, small, win, wout, send, dx_o, final_o, gb1_o
):
    gain, shift, gate, wbias = vectors(small)
    for r in range(2):
        for c in range(2):
            final_o[pl.ds(r * 128 + c, 64, stride=2), :] = recv[pl.ds(12 + 2 * r + c, 64, stride=16), :]
    summed = jnp.sum(recv[...].reshape(64, 16, 128)[:, 4:12, :], axis=0)
    unit1, root1 = norm_parts(first[...])
    y1 = unit1 * gain[1:2, :] + shift[1:2, :]
    dy1 = jnp.concatenate([dot(summed[4 * r : 4 * r + 4], wbias[1], 0, 0) for r in range(2)])
    gb1 = dot(summed[0:4], y1[:128], 1, 0) + dot(summed[4:8], y1[128:], 1, 0)
    up = jnp.concatenate([gather_rows(recv, (2 * r, 2 * r + 1), 16) for r in range(2)])
    up = up + norm_back(dy1, gain[1:2, :], unit1, root1)
    unit, root = norm_parts(xin[...])
    y = unit * gain[0:1, :] + shift[0:1, :]
    proj = proj_s[...]
    mixed = mixed_s[...]
    sig = jax.nn.sigmoid(proj[:, 384:512] + gate[0:1, :])
    dgated = dot(up, wout[0], 1, 1)
    dout = dot(sig * mixed, up, 0, 0)
    dmixed = dgated * sig
    dgate = dgated * mixed * sig * (1.0 - sig)
    dproj, dbias = [], 0.0
    for r in range(2):
        part = proj[r * 128 : r * 128 + 128]
        ds, dq, dk, dv = attention_back(
            dmixed[r * 128 : r * 128 + 128],
            part[:, 0:128],
            part[:, 128:256],
            part[:, 256:384],
            probs_s[r * 512 : r * 512 + 512, :],
            False,
        )
        dbias = dbias + ds
        dproj.append(jnp.concatenate([dq, dk, dv, dgate[r * 128 : r * 128 + 128]], axis=1))
    dproj = jnp.concatenate(dproj)
    din = dot(y, dproj, 0, 0)
    dx_o[...] = up + norm_back(dot(dproj, win[0], 1, 1), gain[0:1, :], unit, root)
    for h in range(4):
        scatter_rows(send, (h, 4 + h), 28, dbias[h * 128 : h * 128 + 128])
    for i in range(10):
        source = din[64 * (i % 2) : 64 * (i % 2) + 64, 128 * (i // 2) : 128 * (i // 2) + 128] if i < 8 else dout[64 * (i - 8) : 64 * (i - 8) + 64]
        send[pl.ds(8 + i, 64, stride=28), :] = source
        send[pl.ds(18 + i, 64, stride=28), :] = wgrad[64 * i : 64 * i + 64, :]
    gb1_o[0:4, :] = gb1
    gb1_o[4:8, :] = gb1


def fourth_kernel(recv, x, gb1, small, shares, totals):
    gain, shift, _, _ = vectors(small)
    pair_sum = jnp.sum(recv[...].reshape(32, 56, 128), axis=0)
    total = pair_sum[0:28] + pair_sum[28:56]
    unit, root = norm_parts(x[...])
    y = unit * gain[0:1, :] + shift[0:1, :]
    gb0 = dot(total[0:4], y[:128], 1, 0) + dot(total[4:8], y[128:], 1, 0)
    totals[...] = total[0:8]
    share = jnp.concatenate([total[8:28], gb0, gb1[0:4, :], jnp.zeros((4, 128), f32)], axis=0) * (1.0 / 128)
    for k in range(4):
        shares[32 * k : 32 * k + 32, :] = share


def tail_kernel(shares, totals, x, dx_s, final, small, share, done):
    gain, _, _, wbias = vectors(small)
    unit, root = norm_parts(x[...])
    dy = jnp.concatenate([dot(totals[4 * r : 4 * r + 4, :], wbias[0], 0, 0) for r in range(2)])
    dx = dx_s[...] + norm_back(dy, gain[0:1, :], unit, root)
    for r in range(2):
        scatter_rows(done, (r * 128, r * 128 + 1), 2, dx[r * 128 : r * 128 + 128])
    done[256:512, :] = final[...]
    for k in range(4):
        share[20 * k : 20 * k + 20, :] = shares[32 * k : 32 * k + 20, :]
    share[80:88, :] = jnp.sum(shares[...].reshape(4, 32, 128)[:, 20:28, :], axis=0)


def spread_kernel(share, out):
    for b in range(16):
        out[88 * b : 88 * b + 88, :] = share[...]


def emit_kernel(done, grad_o, final_o, mark):
    grad_o[...] = done[0:256, :]
    final_o[...] = done[256:512, :]
    mark[...] = done[0:8, :]


def last_kernel(recv, mark, gin, gbias, gout, rows):
    for j in range(20):
        for k in range(4):
            rows[pl.ds(64 * j + k, 16, stride=4), :] = recv[pl.ds(20 * k + j, 16, stride=88), :]
    for m in range(2):
        for e in range(4):
            first = 640 * m + 128 * e
            gin[m, :, 128 * e : 128 * e + 128] = rows[first : first + 128, :]
        gout[m] = rows[640 * m + 512 : 640 * m + 640, :]
    both_bias = jnp.sum(recv[...].reshape(16, 88, 128), axis=0)[80:88]
    gbias[0] = both_bias[0:4]
    gbias[1] = both_bias[4:8]


def call(kernel, outs, *args, cost=None, scratch=()):
    return pl.pallas_call(
        kernel,
        out_shape=tuple(jax.ShapeDtypeStruct(s, f32) for s in outs),
        in_specs=[pl.BlockSpec(memory_space=pltpu.VMEM)] * len(args),
        out_specs=tuple(pl.BlockSpec(memory_space=pltpu.VMEM) for _ in outs),
        scratch_shapes=scratch,
        cost_estimate=cost,
        compiler_params=pltpu.CompilerParams(vmem_limit_bytes=28 * 1024 * 1024),
    )(*args)


def solution(mesh):
    placed, there, back, fours, planes = plans(mesh)

    def swap(a, groups):
        each = a.shape[0] // len(groups[0])
        tile = 8 if each % 8 == 0 else 4
        cut = a.reshape(a.shape[0] // tile, tile, 128) if tile == 4 else a.reshape(-1, each, 128)
        got = lax.all_to_all(cut, both, 0, 0, axis_index_groups=groups, tiled=True)
        return got.reshape(a.shape)

    def body(pair, cotangent, gain, shift, win, wb, gate, wout):
        pair, cotangent = pair.reshape(256, 128), cotangent.reshape(256, 128)
        wbias = jnp.transpose(wb, (0, 2, 1))
        bias, small, packed = pl.pallas_call(
            start_kernel,
            out_shape=(
                jax.ShapeDtypeStruct((8, 128), f32),
                jax.ShapeDtypeStruct((16, 128), f32),
                jax.ShapeDtypeStruct((512, 128), f32),
            ),
            in_specs=[pl.BlockSpec(memory_space=pl.ANY)] * 6,
            out_specs=(
                pl.BlockSpec(memory_space=pltpu.VMEM),
                pl.BlockSpec(memory_space=pltpu.VMEM),
                pl.BlockSpec(memory_space=pl.ANY),
            ),
            scratch_shapes=[
                pltpu.VMEM((512, 128), f32),
                pltpu.VMEM((2, 128), f32),
                pltpu.VMEM((2, 128), f32),
                pltpu.VMEM((2, 128), f32),
                pltpu.VMEM((2, 4, 128), f32),
                pltpu.SemaphoreType.DMA((7,)),
            ],
            compiler_params=pltpu.CompilerParams(vmem_limit_bytes=60 * 1024 * 1024),
        )(pair, cotangent, gain, shift, gate, wbias)
        bias = lax.ppermute(bias, both, there)
        xin = lax.ppermute(packed, both, there)
        (repeated,) = call(repeat_kernel, [(512, 128)], bias, cost=LONG)
        brecv = swap(repeated, placed)
        x, proj, logits = call(
            project_kernel,
            [(256, 128), (256, 512), (1024, 128)],
            *(xin, small, win),
            cost=LONG,
        )
        send1, probs, mixed, first = call(
            first_kernel,
            [(1024, 128), (1024, 128), (256, 128), (256, 128)],
            *(x, xin, brecv, proj, logits, small, wout),
        )
        recv1 = swap(send1, placed)
        send2, wgrad = call(
            second_kernel, [(1024, 128), (640, 128)], recv1, small, win, wout
        )
        recv2 = swap(send2, placed)
        send3, dx, final, gb1 = call(
            third_kernel,
            [(1792, 128), (256, 128), (256, 128), (8, 128)],
            *(recv2, x, first, proj, probs, mixed, wgrad, small, win, wout),
        )
        recv3 = swap(send3, placed)
        shares, totals = call(
            fourth_kernel, [(128, 128), (8, 128)], recv3, x, gb1, small
        )
        share, done = call(
            tail_kernel,
            [(88, 128), (512, 128)],
            *(swap(shares, fours), totals, x, dx, final, small),
        )
        share = lax.ppermute(share, both, back)
        done = lax.ppermute(done, both, back)
        (spread,) = call(spread_kernel, [(1408, 128)], share, cost=LONG)
        recv4 = swap(spread, planes)
        grad, final, mark = call(
            emit_kernel, [(256, 128), (256, 128), (8, 128)], done, cost=LONG
        )
        gin, gbias, gout = call(
            last_kernel,
            [(2, 128, 512), (2, 4, 128), (2, 128, 128)],
            *(recv4, mark),
            scratch=[pltpu.VMEM((1280, 128), f32)],
        )
        return (
            final.reshape(2, 128, 128),
            grad.reshape(2, 128, 128),
            gin,
            jnp.transpose(gbias, (0, 2, 1)),
            gout,
        )

    rows = P(("dp", "axial"), None, None)
    part = P("dp", None, None)
    return jax.shard_map(
        body,
        mesh=mesh,
        in_specs=(rows, rows, P(), P(), P(), P(), P(), P()),
        out_specs=(rows, rows, part, part, part),
        check_vma=False,
    )
```
